1024 devices in a mesh: dp: 64 (over x, y), mp: 16 (over z, core).
Axes of the slice: x: 8, y: 8, z: 8, core: 2. Of those that a mesh axis runs over, the one named last changes fastest.
Arguments:
- query_rows: bfloat16 [32768, 4096], P('dp', 'mp'), may hold values from -6 to 6
- key_rows: bfloat16 [32768, 4096], P('dp', 'mp'), may hold values from -6 to 6
- value_rows: bfloat16 [32768, 4096], P('dp', 'mp'), may hold values from -6 to 6
- out_grad: bfloat16 [32768, 6144], P('dp', 'mp'), may hold values from -6 to 6
- out_weight: bfloat16 [4096, 6144], P('mp'), may hold values from -0.078125 to 0.078125
- destinations: int32 [32768], P('dp'), may hold values from 0 to 63, as said below
- image_ids: int32 [32768], P('dp'), may hold values from 0 to 2, as said below
- patch_counts: int32 [192], P('dp'), may hold values from 2 to 256, as said below
Outputs:
- query_grad: bfloat16 [32768, 4096], P('dp', 'mp')
- key_grad: bfloat16 [32768, 4096], P('dp', 'mp')
- value_grad: bfloat16 [32768, 4096], P('dp', 'mp')
The draws below stay inside these ranges and needn't reach their ends.
Inputs may be any that keep to these rules, and one draw needn't show every extreme that they name: `destinations`: each device holds its tokens as 64 contiguous runs, each run of one image with one destination. Two runs stay on the device; the others go one to each other device but one. Two devices that exchange tokens send each other equally many. The tokens of one device with one other destination are at least 2 and at most 3, and some pair reaches 3; every device is the destination of exactly 512 tokens. `image_ids`: two images of each device lie whole on it; the third is made of the runs that the other devices send to it. patch_counts[d * 3 + k] is the number of tokens with destination d and image id k; each device has one image of exactly 256 patches.
All inputs are finite; a program needn't handle non-finite values.
Results may differ from the reference program's by a relative error of at most 0.015.
Values may be sent and summed in bfloat16 or wider, within the bound.
No kernel may reach another device: no remote copies, remote signals or barrier semaphores. Data moves between devices by JAX's collectives and lax.ppermute only.
A program may use at most 64 MiB of HBM per device.

```python
import jax
import jax.numpy as jnp
from jax import lax

D = 6144
HD = 128
TOK_DEV = 512
IMG_DEV = 3
MINP = 2
CAP = 3
HEADS = 32
TOKENS = 32768
PMAX = 256
N_DP = 64


def structure(key):
    sub_keys = jax.random.split(jax.random.fold_in(key, 5), 6)
    device = jnp.arange(N_DP, dtype=jnp.int32)
    cycle = jax.random.permutation(sub_keys[0], N_DP).astype(jnp.int32)
    place = jnp.argsort(cycle).astype(jnp.int32)
    half = N_DP // 2 - 1
    offsets = jnp.arange(1, half + 1, dtype=jnp.int32)
    sizes = jax.random.randint(sub_keys[1], (half, N_DP), MINP, CAP + 1).astype(jnp.int32)
    sizes = sizes.at[0, 0].set(CAP)
    offset_row = jnp.arange(half, dtype=jnp.int32)[None, :]
    fwd_sizes = sizes[offset_row, place[:, None]]
    back_sizes = sizes[offset_row, (place[:, None] - offsets[None, :]) % N_DP]
    moved = jnp.sum(fwd_sizes, 1) + jnp.sum(back_sizes, 1)
    kept_rest = TOK_DEV - PMAX - moved
    fwd_dev = cycle[(place[:, None] + offsets[None, :]) % N_DP]
    back_dev = cycle[(place[:, None] - offsets[None, :]) % N_DP]
    placing = jax.vmap(lambda part_key: jax.random.permutation(part_key, IMG_DEV))(jax.random.split(sub_keys[4], N_DP)).astype(jnp.int32)
    held_sizes = jnp.concatenate([jnp.full((N_DP, 1), PMAX, jnp.int32), kept_rest[:, None], fwd_sizes, back_sizes], 1).astype(jnp.int32)
    held_dest = jnp.concatenate([device[:, None], device[:, None], fwd_dev, back_dev], 1).astype(jnp.int32)
    held_id = jnp.concatenate([placing[device, 0][:, None], placing[device, 1][:, None], placing[fwd_dev, 2], placing[back_dev, 2]], 1).astype(jnp.int32)
    dest_sizes = jnp.stack([jnp.full((N_DP,), PMAX, jnp.int32), kept_rest, moved], 1).astype(jnp.int32)
    lengths = jnp.zeros((N_DP, IMG_DEV), jnp.int32).at[device[:, None], placing].set(dest_sizes)
    order = jax.vmap(lambda part_key: jax.random.permutation(part_key, N_DP))(jax.random.split(sub_keys[5], N_DP)).astype(jnp.int32)
    run_sizes = jnp.take_along_axis(held_sizes, order, 1)
    run_ends = jnp.cumsum(run_sizes, 1).astype(jnp.int32)
    position = jnp.arange(TOK_DEV, dtype=jnp.int32)
    run_index = jax.vmap(lambda ends: jnp.searchsorted(ends, position, side='right'))(run_ends).astype(jnp.int32)
    slot = jnp.take_along_axis(order, run_index, 1)
    targets = jnp.take_along_axis(held_dest, slot, 1)
    local_ids = jnp.take_along_axis(held_id, slot, 1)
    return (targets.reshape(TOK_DEV * N_DP).astype(jnp.int32), local_ids.reshape(TOK_DEV * N_DP).astype(jnp.int32), lengths.reshape(N_DP * IMG_DEV).astype(jnp.int32))


def draw_destinations(key, part):
    return structure(key)[0]


def draw_image_ids(key, part):
    return structure(key)[1]


def draw_patch_counts(key, part):
    return structure(key)[2]


def draw_query_rows(key, part):
    key = jax.random.fold_in(key, 21)
    drawn = jnp.clip(jax.random.normal(key, (TOKENS, HEADS * HD), jnp.float32), -6.0, 6.0)
    return drawn.astype(jnp.bfloat16)


def draw_key_rows(key, part):
    key = jax.random.fold_in(key, 22)
    drawn = jnp.clip(jax.random.normal(key, (TOKENS, HEADS * HD), jnp.float32), -6.0, 6.0)
    return drawn.astype(jnp.bfloat16)


def block_levels(key, shape, shards, low, top_value):
    factor_of = 1.0
    for dim, shards_of in shards:
        draws = jax.random.uniform(jax.random.fold_in(jax.random.fold_in(key, 6), dim), (shards_of,), jnp.float32, low / len(shards), top_value / len(shards))
        factor_of = factor_of * jnp.repeat(jnp.exp(draws), shape[dim] // shards_of).reshape((-1,) + (1,) * (len(shape) - 1 - dim))
    return factor_of


def normal_values(stream_key, extent, spread, bound, cuts=(), held_as=jnp.bfloat16):
    result = jax.random.normal(stream_key, extent, jnp.float32) * spread
    if len(cuts) > 0:
        result = block_levels(stream_key, extent, cuts, -0.22, 0.18) * result
    return jnp.clip(result, min=-bound, max=bound).astype(held_as)


def setup_inputs(seed: int = 0) -> dict:
    keys = jax.random.split(jax.random.key(seed), 9)
    query_rows = draw_query_rows(jax.random.fold_in(keys[8], 71), 0)
    key_rows = draw_key_rows(jax.random.fold_in(keys[8], 71), 0)
    value_rows = normal_values(keys[2], (TOKENS, HEADS * HD), 1.0, 6.0, ((0, 64), (1, 16)))
    out_grad = normal_values(keys[3], (TOKENS, D), 1.0, 6.0, ((0, 64), (1, 16)))
    out_weight = normal_values(keys[4], (HEADS * HD, D), D ** -0.5, 0.078125, ((0, 16),))
    destinations = draw_destinations(jax.random.fold_in(keys[8], 71), 0)
    image_ids = draw_image_ids(jax.random.fold_in(keys[8], 71), 0)
    patch_counts = draw_patch_counts(jax.random.fold_in(keys[8], 71), 0)
    return dict(query_rows=query_rows, key_rows=key_rows, value_rows=value_rows, out_grad=out_grad, out_weight=out_weight, destinations=destinations, image_ids=image_ids, patch_counts=patch_counts)


def attend(query_part, key_part, value_part, grad_part, id_part, row_weight):
    score_scale = 1.0 / (query_part.shape[-1] ** 0.5)
    query_f = query_part.astype(jnp.float32)
    key_f = key_part.astype(jnp.float32)
    value_f = value_part.astype(jnp.float32)
    grad_f = grad_part.astype(jnp.float32)
    scores = jnp.einsum("ihc,jhc->hij", query_f, key_f) * score_scale
    same_image = id_part[:, None] == id_part[None, :]
    scores = jnp.where(same_image[None], scores, -jnp.inf)
    row_max = jnp.max(scores, axis=-1, keepdims=True)
    raised = jnp.exp(scores - row_max)
    probs = raised / jnp.sum(raised, axis=-1, keepdims=True)
    probs_low = probs.astype(jnp.bfloat16)
    attended = jnp.einsum("hij,jhc->ihc", probs_low.astype(jnp.float32), value_f)
    row_dot = jnp.sum(grad_f * attended, axis=-1)
    scaled_probs = row_weight[None, :, None] * probs
    weighted = scaled_probs.astype(jnp.bfloat16)
    value_grad = jnp.einsum("hij,ihc->jhc", weighted.astype(jnp.float32), grad_f).astype(jnp.bfloat16)
    prob_grad = jnp.einsum("ihc,jhc->hij", grad_f, value_f)
    score_grad = (scaled_probs * (prob_grad - jnp.transpose(row_dot)[:, :, None])).astype(jnp.bfloat16)
    score_f = score_grad.astype(jnp.float32)
    query_grad = (jnp.einsum("hij,jhc->ihc", score_f, key_f) * score_scale).astype(jnp.bfloat16)
    key_grad = (jnp.einsum("hij,ihc->jhc", score_f, query_f) * score_scale).astype(jnp.bfloat16)
    return query_grad, key_grad, value_grad


def reference(query_rows, key_rows, value_rows, out_grad, out_weight, destinations, image_ids, patch_counts):
    attn_grad = jnp.dot(out_grad, out_weight.T, preferred_element_type=jnp.float32).astype(jnp.bfloat16)
    image_index = (destinations * IMG_DEV + image_ids).astype(jnp.int32)
    counts = patch_counts[image_index].astype(jnp.float32)
    row_weight = TOK_DEV / (IMG_DEV * counts)
    ordering = jnp.argsort(destinations, stable=True).astype(jnp.int32)
    groups = ordering.reshape(N_DP, TOK_DEV)
    head_count = query_rows.shape[1] // HD

    def per_group(index_set):
        def pick(source):
            return source[index_set].reshape(TOK_DEV, head_count, HD)
        results = attend(pick(query_rows), pick(key_rows), pick(value_rows), pick(attn_grad), image_ids[index_set], row_weight[index_set])
        return tuple(part.reshape(TOK_DEV, head_count * HD) for part in results)

    grouped = lax.map(per_group, groups)
    flat_order = groups.reshape(TOKENS)
    outputs = []
    for part in grouped:
        empty = jnp.zeros((TOKENS, head_count * HD), jnp.bfloat16)
        outputs.append(empty.at[flat_order].set(part.reshape(TOKENS, head_count * HD)))
    return outputs[0], outputs[1], outputs[2]
```

```python
import functools
import math

import jax
import jax.numpy as jnp
from jax import lax
from jax.experimental import pallas as pl
from jax.experimental.pallas import tpu as pltpu
from jax.sharding import PartitionSpec as P

HD = 128
CAP = 3
BIG = 256
SMALL = 144
KEPT = BIG + SMALL
OCT = 8
LOG2E = 1.4426950408889634
F32 = jnp.float32
BF16 = jnp.bfloat16
MIB = 1024 * 1024
NT = (((1,), (1,)), ((), ()))
TN = (((0,), (0,)), ((), ()))


def iota(shape, dim):
    return lax.broadcasted_iota(jnp.int32, shape, dim)


def one_hot(cond):
    return jnp.where(cond, 1.0, 0.0).astype(BF16)


def pick(hot, rows):
    return jnp.dot(hot, rows, preferred_element_type=F32).astype(BF16)


def slot_row(slot, n_dp):
    return OCT * (slot % n_dp) + 2 * (slot // n_dp)


def plan_kernel(n_dp, dest_ref, ids_ref, counts_ref, og_ref, pos_ref, og_moved_ref):
    tok = dest_ref.shape[1]
    slots = n_dp * CAP
    mine = lax.axis_index("dp")
    dest = dest_ref[...]
    counts = counts_ref[...]
    big_id = jnp.where(
        counts[:, 0:1] == BIG, 0, jnp.where(counts[:, 1:2] == BIG, 1, 2)
    )
    kept_class = jnp.where(ids_ref[...] == big_id, n_dp, n_dp + 1)
    group = jnp.where(dest == mine, kept_class, dest)
    n_rows = n_dp + 16
    row = iota((n_rows, tok), 0)
    member = row == group
    before = one_hot(iota((tok, tok), 0) < iota((tok, tok), 1))
    rank = jnp.dot(one_hot(member), before, preferred_element_type=F32)
    start = jnp.where(row < n_dp, row, jnp.where(row == n_dp, slots, slots + BIG))
    step = jnp.where(row < n_dp, float(n_dp), 1.0)
    place = jnp.where(member, start.astype(F32) + step * rank, 0.0)
    pos = jnp.sum(place, axis=0, keepdims=True).astype(jnp.int32)
    pos_ref[...] = jnp.broadcast_to(pos, pos_ref.shape)
    og_moved_ref[...] = pick(one_hot(iota((slots, tok), 0) == pos), og_ref[...])


def pack_kernel(
    n_dp, pos_ref, og_ref, q_ref, k_ref, v_ref,
    send_ref, og_kept_ref, rows_kept_ref, used_ref, kept_used_ref, pos_col_ref,
):
    tok = og_ref.shape[0]
    slots = n_dp * CAP
    pos = pos_ref[0:1, :]
    q, k, v = q_ref[...], k_ref[...], v_ref[...]
    first = jnp.where(pos < slots, slot_row(pos, n_dp), -OCT)
    row = iota((n_dp * OCT, tok), 0)
    left = jnp.concatenate([q, k[:, :HD]], 1)
    right = jnp.concatenate([k[:, HD:], v], 1)
    send_ref[...] = (
        jnp.dot(one_hot(row == first), left, preferred_element_type=F32)
        + jnp.dot(one_hot(row == first + 1), right, preferred_element_type=F32)
    ).astype(BF16)
    kept_hot = one_hot(iota((KEPT, tok), 0) + slots == pos)
    og_kept_ref[...] = pick(kept_hot, og_ref[...])
    rows_kept_ref[...] = pick(kept_hot, jnp.concatenate([q, k, v], 1))
    ones = jnp.ones((tok, HD), BF16)
    slot_hot = one_hot(iota((slots, tok), 0) == pos)
    used_ref[...] = jnp.dot(slot_hot, ones, preferred_element_type=F32)
    kept_used_ref[...] = jnp.dot(kept_hot[BIG:], ones, preferred_element_type=F32)
    wide = jnp.broadcast_to(pos.astype(F32), (HD, tok))
    pos_col_ref[...] = jnp.transpose(wide).astype(jnp.int32)


def attend(q, k, v, g, valid, weight):
    scale = 1.0 / HD**0.5
    scores = lax.dot_general(k, q, NT, preferred_element_type=F32)
    if valid is not None:
        scores = jnp.where(valid, scores, -1e30)
    top = jnp.max(scores, axis=0, keepdims=True)
    raised = jnp.exp2((scores - top) * (scale * LOG2E))
    total = jnp.sum(raised, axis=0, keepdims=True)
    probs = raised * (1.0 / total)
    prob_grad = lax.dot_general(v, g, NT, preferred_element_type=F32)
    row_dot = jnp.sum(probs * prob_grad, axis=0, keepdims=True)
    scaled = probs * weight
    value_grad = jnp.dot(scaled.astype(BF16), g, preferred_element_type=F32)
    score_grad = (scaled * (prob_grad - row_dot)).astype(BF16)
    key_grad = jnp.dot(score_grad, q, preferred_element_type=F32) * scale
    query_grad = lax.dot_general(score_grad, k, TN, preferred_element_type=F32) * scale
    return query_grad.astype(BF16), key_grad.astype(BF16), value_grad.astype(BF16)


def block_dot(rows, w_ref, start):
    cols = rows.shape[1]
    weight = w_ref[:, pl.ds(pl.multiple_of(start, HD), cols)]
    return lax.dot_general(rows, weight, NT, preferred_element_type=F32)


def partial_kernel(n_mp, own_ref, hop1_ref, hop2_ref, w_ref, w_pair_ref, acc_ref, w_late_ref):
    feat = own_ref.shape[1]
    me = lax.axis_index("mp")
    chips = n_mp // 2
    chip, core = me // 2, me % 2

    def start(away):
        return (jnp.where(core == 0, chip - away, chip + away) + chips) % chips * (2 * feat)

    third = pl.multiple_of(start(3), HD)
    last = pl.multiple_of((me + chips) % n_mp * feat, HD)
    for side, weight_ref in enumerate((w_ref, w_pair_ref)):
        acc = block_dot(own_ref[...], weight_ref, me * feat)
        for away, hop_ref in ((1, hop1_ref), (2, hop2_ref)):
            for half in range(2):
                acc = acc + block_dot(hop_ref[half], weight_ref, start(away) + half * feat)
        acc_ref[side] = acc
        w_late_ref[side, :, : 2 * feat] = weight_ref[:, pl.ds(third, 2 * feat)]
        w_late_ref[side, :, 2 * feat :] = weight_ref[:, pl.ds(last, feat)]


def last_kernel(acc_ref, hop3_ref, hop4_ref, w_late_ref, mine_ref, pair_ref):
    feat = hop4_ref.shape[2]
    for side, out in enumerate((mine_ref, pair_ref)):
        acc = acc_ref[side]
        for part, rows in enumerate((hop3_ref[0], hop3_ref[1], hop4_ref[0])):
            weight = w_late_ref[side, :, part * feat : (part + 1) * feat]
            acc = acc + lax.dot_general(rows, weight, NT, preferred_element_type=F32)
        out[...] = acc


def spread(n_dp, half, slots):
    shape = (n_dp * OCT, slots)
    return one_hot(iota(shape, 0) == slot_row(iota(shape, 1), n_dp) + half)


def moved_kernel(n_dp, mine_ref, pair_ref, send_ref):
    slots = n_dp * CAP
    grad = (mine_ref[...] + pair_ref[...]).astype(BF16)
    send_ref[...] = (
        jnp.dot(spread(n_dp, 0, slots), grad[:, :HD], preferred_element_type=F32)
        + jnp.dot(spread(n_dp, 1, slots), grad[:, HD:], preferred_element_type=F32)
    ).astype(BF16)


def remote_kernel(n_dp, tok, img, rows_ref, grad_ref, valid_ref, send_ref):
    slots = n_dp * CAP
    shape = (slots, n_dp * OCT)
    first = slot_row(iota(shape, 0), n_dp)
    hot0 = one_hot(iota(shape, 1) == first)
    hot1 = one_hot(iota(shape, 1) == first + 1)
    rows, grad = rows_ref[...], grad_ref[...]
    a, b = pick(hot0, rows), pick(hot1, rows)
    g0, g1 = pick(hot0, grad), pick(hot1, grad)
    valid = valid_ref[:, 0:1]
    count = jnp.sum(valid, axis=0, keepdims=True)
    weight = tok / (img * count)
    mask = valid > 0.5
    q0, q1, k0 = a[:, :HD], a[:, HD : 2 * HD], a[:, 2 * HD :]
    k1, v0, v1 = b[:, :HD], b[:, HD : 2 * HD], b[:, 2 * HD :]
    dq0, dk0, dv0 = attend(q0, k0, v0, g0, mask, weight)
    dq1, dk1, dv1 = attend(q1, k1, v1, g1, mask, weight)
    send_ref[...] = (
        jnp.dot(spread(n_dp, 0, slots), jnp.concatenate([dq0, dq1, dk0], 1), preferred_element_type=F32)
        + jnp.dot(spread(n_dp, 1, slots), jnp.concatenate([dk1, dv0, dv1], 1), preferred_element_type=F32)
    ).astype(BF16)


def local_kernel(
    n_dp, tok, img, mine_ref, pair_ref, rows_ref, valid_ref, pos_ref, dq_ref, dk_ref, dv_ref
):
    slots = n_dp * CAP
    grad = (mine_ref[...] + pair_ref[...]).astype(BF16)
    valid = valid_ref[:, 0:1]
    count = jnp.sum(valid, axis=0, keepdims=True)
    images = (
        (slice(0, BIG), None, tok / (img * BIG)),
        (slice(BIG, KEPT), valid > 0.5, tok / (img * count)),
    )
    parts = []
    for head in range(2):
        lanes = slice(head * HD, (head + 1) * HD)
        pieces = []
        for span, mask, weight in images:
            q = rows_ref[span, head * HD : (head + 1) * HD]
            k = rows_ref[span, (2 + head) * HD : (3 + head) * HD]
            v = rows_ref[span, (4 + head) * HD : (5 + head) * HD]
            pieces.append(attend(q, k, v, grad[span, lanes], mask, weight))
        parts.append([jnp.concatenate(p, 0) for p in zip(*pieces)])
    pos = pos_ref[:, 0:1] - slots
    hot = one_hot(iota((tok, KEPT), 1) == pos)
    for name, out in enumerate((dq_ref, dk_ref, dv_ref)):
        out[...] = pick(hot, jnp.concatenate([parts[0][name], parts[1][name]], 1))


def merge_kernel(n_dp, back_ref, pos_ref, q_ref, k_ref, v_ref, dq_ref, dk_ref, dv_ref):
    tok = q_ref.shape[0]
    slots = n_dp * CAP
    pos = pos_ref[:, 0:1]
    first = jnp.where(pos < slots, slot_row(pos, n_dp), -OCT)
    col = iota((tok, n_dp * OCT), 1)
    back = back_ref[...]
    a = pick(one_hot(col == first), back)
    b = pick(one_hot(col == first + 1), back)
    dq_ref[...] = q_ref[...] + a[:, : 2 * HD]
    dk_ref[...] = k_ref[...] + jnp.concatenate([a[:, 2 * HD :], b[:, :HD]], 1)
    dv_ref[...] = v_ref[...] + b[:, HD:]


def sds(shape, dtype):
    return jax.ShapeDtypeStruct(shape, dtype)


def call(kernel, ins, outs, name, vmem=56, flops=0):
    def whole(x):
        zeros = (0,) * len(x.shape)
        return pl.BlockSpec(x.shape, lambda i: zeros)

    many = isinstance(outs, tuple)
    moved = sum(math.prod(x.shape) * x.dtype.itemsize for x in (*ins, *(outs if many else (outs,))))
    return pl.pallas_call(
        kernel,
        out_shape=outs,
        grid=(1,),
        in_specs=[whole(x) for x in ins],
        out_specs=tuple(whole(x) for x in outs) if many else whole(outs),
        compiler_params=pltpu.CompilerParams(vmem_limit_bytes=vmem * MIB),
        cost_estimate=pl.CostEstimate(flops=flops, bytes_accessed=moved, transcendentals=0),
        name=name,
    )(*ins)


def local(
    query_rows, key_rows, value_rows, out_grad, out_weight, destinations, image_ids, patch_counts
):
    tok, cols = query_rows.shape
    feat = out_grad.shape[1]
    n_dp, n_mp = lax.axis_size("dp"), lax.axis_size("mp")
    slots = n_dp * CAP
    img = patch_counts.shape[0]
    exch = n_dp * OCT
    pairs = [[2 * i, 2 * i + 1] for i in range(n_mp // 2)]
    swap = [(i, i ^ 1) for i in range(n_mp)]
    ring = [(i, (i + (2 if i % 2 == 0 else -2)) % n_mp) for i in range(n_mp)]

    def exchange(rows):
        shaped = rows.reshape(n_dp, OCT, rows.shape[1])
        return lax.all_to_all(shaped, "dp", split_axis=0, concat_axis=0, tiled=True).reshape(rows.shape)

    def after(value, earlier):
        return lax.optimization_barrier((value, earlier))[0]

    def hop(block):
        return lax.ppermute(block, "mp", ring)

    def both_cores(rows):
        return lax.all_gather(rows, "mp", axis=0, axis_index_groups=pairs)

    def opposite(block):
        half = lax.dynamic_slice_in_dim(block, lax.axis_index("mp") % 2, 1, 0)
        return hop(half)

    def projected(own, hop1, hop2):
        return call(
            functools.partial(partial_kernel, n_mp),
            (own, hop1, hop2, out_weight, pair_weight),
            (sds((2, own.shape[0], cols), F32), sds((2, cols, 3 * feat), BF16)),
            "partial",
        )

    def finished(acc, w_late, hop3, hop4):
        mine, pair = call(
            last_kernel, (acc, hop3, hop4, w_late), (sds((hop4.shape[1], cols), F32),) * 2, "last"
        )
        return mine, lax.ppermute(pair, "mp", swap)

    pair_weight = lax.ppermute(out_weight, "mp", swap)
    pos, og_moved = call(
        functools.partial(plan_kernel, n_dp),
        (destinations.reshape(1, tok), image_ids.reshape(1, tok), patch_counts.reshape(1, img), out_grad),
        (sds((8, tok), jnp.int32), sds((slots, feat), BF16)),
        "plan",
    )
    hop1 = hop(both_cores(og_moved))
    send, og_kept, rows_kept, used, kept_used, pos_col = call(
        functools.partial(pack_kernel, n_dp),
        (pos, out_grad, query_rows, key_rows, value_rows),
        (
            sds((exch, 3 * HD), BF16),
            sds((KEPT, feat), BF16),
            sds((KEPT, 3 * cols), BF16),
            sds((slots, HD), F32),
            sds((SMALL, HD), F32),
            sds((tok, HD), jnp.int32),
        ),
        "pack",
    )
    kept_block = both_cores(og_kept)
    rows_in = exchange(send)
    hop2 = hop(after(hop1, send))
    hop3 = hop(hop2)
    acc, w_late = projected(og_moved, hop1, hop2)
    hop4 = opposite(after(hop3, acc))
    kept1 = hop(after(kept_block, hop4))
    mine, pair = finished(acc, w_late, hop3, hop4)
    pair = after(pair, rows_in)
    grad_send = call(
        functools.partial(moved_kernel, n_dp), (mine, pair), sds((exch, HD), BF16), "moved", 8
    )
    grad_in = exchange(grad_send)
    kept2 = hop(after(kept1, grad_send))
    kept3 = hop(after(kept2, grad_in))
    back_send = call(
        functools.partial(remote_kernel, n_dp, tok, img),
        (rows_in, grad_in, used),
        sds((exch, 3 * HD), BF16),
        "remote",
        12,
    )
    back = exchange(back_send)
    kept4 = opposite(after(kept3, back_send))
    mine, pair = finished(*projected(og_kept, kept1, kept2), kept3, kept4)
    kept_grads = call(
        functools.partial(local_kernel, n_dp, tok, img),
        (mine, pair, rows_kept, kept_used, pos_col),
        (sds((tok, cols), BF16),) * 3,
        "kept",
        24,
    )
    return call(
        functools.partial(merge_kernel, n_dp),
        (back, pos_col) + kept_grads,
        (sds((tok, cols), BF16),) * 3,
        "merge",
        12,
    )


def solution(mesh):
    rows = P("dp", "mp")
    return jax.shard_map(
        local,
        mesh=mesh,
        in_specs=(rows, rows, rows, rows, P("mp", None), P("dp"), P("dp"), P("dp")),
        out_specs=(rows, rows, rows),
        check_vma=False,
    )
```

```python
import functools
import math

import jax
import jax.numpy as jnp
from jax import lax
from jax.experimental import pallas as pl
from jax.experimental.pallas import tpu as pltpu
from jax.sharding import PartitionSpec as P

HD = 128
CAP = 3
BIG = 256
SMALL = 144
KEPT = BIG + SMALL
OCT = 8
LOG2E = 1.4426950408889634
F32 = jnp.float32
BF16 = jnp.bfloat16
MIB = 1024 * 1024
NT = (((1,), (1,)), ((), ()))
TN = (((0,), (0,)), ((), ()))


def iota(shape, dim):
    return lax.broadcasted_iota(jnp.int32, shape, dim)


def one_hot(cond):
    return jnp.where(cond, 1.0, 0.0).astype(BF16)


def pick(hot, rows):
    return jnp.dot(hot, rows, preferred_element_type=F32).astype(BF16)


def slot_row(slot, n_dp):
    return OCT * (slot % n_dp) + 2 * (slot // n_dp)


def plan_kernel(n_dp, dest_ref, ids_ref, counts_ref, og_ref, pos_ref, og_moved_ref):
    tok = dest_ref.shape[1]
    slots = n_dp * CAP
    mine = lax.axis_index("dp")
    dest = dest_ref[...]
    counts = counts_ref[...]
    big_id = jnp.where(
        counts[:, 0:1] == BIG, 0, jnp.where(counts[:, 1:2] == BIG, 1, 2)
    )
    kept_class = jnp.where(ids_ref[...] == big_id, n_dp, n_dp + 1)
    group = jnp.where(dest == mine, kept_class, dest)
    n_rows = n_dp + 16
    row = iota((n_rows, tok), 0)
    member = row == group
    before = one_hot(iota((tok, tok), 0) < iota((tok, tok), 1))
    rank = jnp.dot(one_hot(member), before, preferred_element_type=F32)
    start = jnp.where(row < n_dp, row, jnp.where(row == n_dp, slots, slots + BIG))
    step = jnp.where(row < n_dp, float(n_dp), 1.0)
    place = jnp.where(member, start.astype(F32) + step * rank, 0.0)
    pos = jnp.sum(place, axis=0, keepdims=True).astype(jnp.int32)
    pos_ref[...] = jnp.broadcast_to(pos, pos_ref.shape)
    rows = pick(one_hot(iota((slots, tok), 0) == pos), og_ref[...])
    for copy in range(og_moved_ref.shape[0]):
        og_moved_ref[copy] = rows


def pack_kernel(
    n_dp, pos_ref, og_ref, q_ref, k_ref, v_ref,
    send_ref, og_kept_ref, rows_kept_ref, used_ref, kept_used_ref, pos_col_ref,
):
    tok = og_ref.shape[0]
    slots = n_dp * CAP
    pos = pos_ref[0:1, :]
    q, k, v = q_ref[...], k_ref[...], v_ref[...]
    first = jnp.where(pos < slots, slot_row(pos, n_dp), -OCT)
    row = iota((n_dp * OCT, tok), 0)
    left = jnp.concatenate([q, k[:, :HD]], 1)
    right = jnp.concatenate([k[:, HD:], v], 1)
    send_ref[...] = (
        jnp.dot(one_hot(row == first), left, preferred_element_type=F32)
        + jnp.dot(one_hot(row == first + 1), right, preferred_element_type=F32)
    ).astype(BF16)
    kept_hot = one_hot(iota((KEPT, tok), 0) + slots == pos)
    og_kept_ref[...] = pick(kept_hot, og_ref[...])
    rows_kept_ref[...] = pick(kept_hot, jnp.concatenate([q, k, v], 1))
    ones = jnp.ones((tok, HD), BF16)
    slot_hot = one_hot(iota((slots, tok), 0) == pos)
    used_ref[...] = jnp.dot(slot_hot, ones, preferred_element_type=F32)
    kept_used_ref[...] = jnp.dot(kept_hot[BIG:], ones, preferred_element_type=F32)
    wide = jnp.broadcast_to(pos.astype(F32), (HD, tok))
    pos_col_ref[...] = jnp.transpose(wide).astype(jnp.int32)


def attend(q, k, v, g, valid, weight):
    scale = 1.0 / HD**0.5
    scores = lax.dot_general(k, q, NT, preferred_element_type=F32)
    if valid is not None:
        scores = jnp.where(valid, scores, -1e30)
    top = jnp.max(scores, axis=0, keepdims=True)
    raised = jnp.exp2((scores - top) * (scale * LOG2E))
    total = jnp.sum(raised, axis=0, keepdims=True)
    probs = raised * (1.0 / total)
    prob_grad = lax.dot_general(v, g, NT, preferred_element_type=F32)
    row_dot = jnp.sum(probs * prob_grad, axis=0, keepdims=True)
    scaled = probs * weight
    value_grad = jnp.dot(scaled.astype(BF16), g, preferred_element_type=F32)
    score_grad = (scaled * (prob_grad - row_dot)).astype(BF16)
    key_grad = jnp.dot(score_grad, q, preferred_element_type=F32) * scale
    query_grad = lax.dot_general(score_grad, k, TN, preferred_element_type=F32) * scale
    return query_grad.astype(BF16), key_grad.astype(BF16), value_grad.astype(BF16)


def block_dot(rows, w_ref, start):
    cols = rows.shape[1]
    weight = w_ref[:, pl.ds(pl.multiple_of(start, HD), cols)]
    return lax.dot_general(rows, weight, NT, preferred_element_type=F32)


def partial_kernel(n_mp, own_ref, hop1_ref, hop2_ref, w_ref, w_pair_ref, acc_ref, w_late_ref):
    feat = own_ref.shape[1]
    me = lax.axis_index("mp")
    chips = n_mp // 2
    chip, core = me // 2, me % 2

    def start(away):
        return (jnp.where(core == 0, chip - away, chip + away) + chips) % chips * (2 * feat)

    third = pl.multiple_of(start(3), HD)
    last = pl.multiple_of((me + chips) % n_mp * feat, HD)
    for side, weight_ref in enumerate((w_ref, w_pair_ref)):
        acc = block_dot(own_ref[...], weight_ref, me * feat)
        for away, hop_ref in ((1, hop1_ref), (2, hop2_ref)):
            for half in range(2):
                acc = acc + block_dot(hop_ref[half], weight_ref, start(away) + half * feat)
        acc_ref[side] = acc
        w_late_ref[side, :, : 2 * feat] = weight_ref[:, pl.ds(third, 2 * feat)]
        w_late_ref[side, :, 2 * feat :] = weight_ref[:, pl.ds(last, feat)]


def last_kernel(acc_ref, hop3_ref, hop4_ref, w_late_ref, mine_ref, pair_ref):
    feat = hop4_ref.shape[2]
    for side, out in enumerate((mine_ref, pair_ref)):
        acc = acc_ref[side]
        for part, rows in enumerate((hop3_ref[0], hop3_ref[1], hop4_ref[0])):
            weight = w_late_ref[side, :, part * feat : (part + 1) * feat]
            acc = acc + lax.dot_general(rows, weight, NT, preferred_element_type=F32)
        out[...] = acc


def spread(n_dp, half, slots):
    shape = (n_dp * OCT, slots)
    return one_hot(iota(shape, 0) == slot_row(iota(shape, 1), n_dp) + half)


def chips_kernel(n_mp, og_ref, w_ref, w_pair_ref, mine_ref, pair_ref):
    chips, _, feat = og_ref.shape
    core = lax.axis_index("mp") % 2
    for weight_ref, out in ((w_ref, mine_ref), (w_pair_ref, pair_ref)):
        acc = block_dot(og_ref[0], weight_ref, core * feat)
        for chip in range(1, chips):
            acc = acc + block_dot(og_ref[chip], weight_ref, (2 * chip + core) * feat)
        out[...] = acc


def moved_kernel(n_dp, mine_ref, pair_ref, rows_ref, send_ref):
    slots = n_dp * CAP
    grad = (mine_ref[...] + pair_ref[...]).astype(BF16)
    send_ref[:, : 3 * HD] = rows_ref[...]
    send_ref[:, 3 * HD :] = (
        jnp.dot(spread(n_dp, 0, slots), grad[:, :HD], preferred_element_type=F32)
        + jnp.dot(spread(n_dp, 1, slots), grad[:, HD:], preferred_element_type=F32)
    ).astype(BF16)


def remote_kernel(n_dp, tok, img, rows_ref, valid_ref, send_ref):
    slots = n_dp * CAP
    shape = (slots, n_dp * OCT)
    first = slot_row(iota(shape, 0), n_dp)
    hot0 = one_hot(iota(shape, 1) == first)
    hot1 = one_hot(iota(shape, 1) == first + 1)
    a, b = pick(hot0, rows_ref[...]), pick(hot1, rows_ref[...])
    valid = valid_ref[:, 0:1]
    count = jnp.sum(valid, axis=0, keepdims=True)
    weight = tok / (img * count)
    mask = valid > 0.5
    q0, q1, k0, g0 = (a[:, i * HD : (i + 1) * HD] for i in range(4))
    k1, v0, v1, g1 = (b[:, i * HD : (i + 1) * HD] for i in range(4))
    dq0, dk0, dv0 = attend(q0, k0, v0, g0, mask, weight)
    dq1, dk1, dv1 = attend(q1, k1, v1, g1, mask, weight)
    send_ref[...] = (
        jnp.dot(spread(n_dp, 0, slots), jnp.concatenate([dq0, dq1, dk0], 1), preferred_element_type=F32)
        + jnp.dot(spread(n_dp, 1, slots), jnp.concatenate([dk1, dv0, dv1], 1), preferred_element_type=F32)
    ).astype(BF16)


def local_kernel(
    n_dp, tok, img, mine_ref, pair_ref, rows_ref, valid_ref, pos_ref, dq_ref, dk_ref, dv_ref
):
    slots = n_dp * CAP
    grad = (mine_ref[...] + pair_ref[...]).astype(BF16)
    valid = valid_ref[:, 0:1]
    count = jnp.sum(valid, axis=0, keepdims=True)
    images = (
        (slice(0, BIG), None, tok / (img * BIG)),
        (slice(BIG, KEPT), valid > 0.5, tok / (img * count)),
    )
    parts = []
    for head in range(2):
        lanes = slice(head * HD, (head + 1) * HD)
        pieces = []
        for span, mask, weight in images:
            q = rows_ref[span, head * HD : (head + 1) * HD]
            k = rows_ref[span, (2 + head) * HD : (3 + head) * HD]
            v = rows_ref[span, (4 + head) * HD : (5 + head) * HD]
            pieces.append(attend(q, k, v, grad[span, lanes], mask, weight))
        parts.append([jnp.concatenate(p, 0) for p in zip(*pieces)])
    pos = pos_ref[:, 0:1] - slots
    hot = one_hot(iota((tok, KEPT), 1) == pos)
    for name, out in enumerate((dq_ref, dk_ref, dv_ref)):
        out[...] = pick(hot, jnp.concatenate([parts[0][name], parts[1][name]], 1))


def merge_kernel(n_dp, back_ref, pos_ref, q_ref, k_ref, v_ref, dq_ref, dk_ref, dv_ref):
    tok = q_ref.shape[0]
    slots = n_dp * CAP
    pos = pos_ref[:, 0:1]
    first = jnp.where(pos < slots, slot_row(pos, n_dp), -OCT)
    col = iota((tok, n_dp * OCT), 1)
    back = back_ref[...]
    a = pick(one_hot(col == first), back)
    b = pick(one_hot(col == first + 1), back)
    dq_ref[...] = q_ref[...] + a[:, : 2 * HD]
    dk_ref[...] = k_ref[...] + jnp.concatenate([a[:, 2 * HD :], b[:, :HD]], 1)
    dv_ref[...] = v_ref[...] + b[:, HD:]


def sds(shape, dtype):
    return jax.ShapeDtypeStruct(shape, dtype)


def call(kernel, ins, outs, name, vmem=56, flops=0):
    def whole(x):
        zeros = (0,) * len(x.shape)
        return pl.BlockSpec(x.shape, lambda i: zeros)

    many = isinstance(outs, tuple)
    moved = sum(math.prod(x.shape) * x.dtype.itemsize for x in (*ins, *(outs if many else (outs,))))
    return pl.pallas_call(
        kernel,
        out_shape=outs,
        grid=(1,),
        in_specs=[whole(x) for x in ins],
        out_specs=tuple(whole(x) for x in outs) if many else whole(outs),
        compiler_params=pltpu.CompilerParams(vmem_limit_bytes=vmem * MIB),
        cost_estimate=pl.CostEstimate(flops=flops, bytes_accessed=moved, transcendentals=0),
        name=name,
    )(*ins)


def local(
    query_rows, key_rows, value_rows, out_grad, out_weight, destinations, image_ids, patch_counts
):
    tok, cols = query_rows.shape
    feat = out_grad.shape[1]
    n_dp, n_mp = lax.axis_size("dp"), lax.axis_size("mp")
    slots = n_dp * CAP
    img = patch_counts.shape[0]
    exch = n_dp * OCT
    pairs = [[2 * i, 2 * i + 1] for i in range(n_mp // 2)]
    swap = [(i, i ^ 1) for i in range(n_mp)]
    ring = [(i, (i + (2 if i % 2 == 0 else -2)) % n_mp) for i in range(n_mp)]

    def exchange(rows):
        shaped = rows.reshape(n_dp, OCT, rows.shape[1])
        return lax.all_to_all(shaped, "dp", split_axis=0, concat_axis=0, tiled=True).reshape(rows.shape)

    def after(value, earlier):
        return lax.optimization_barrier((value, earlier))[0]

    def hop(block):
        return lax.ppermute(block, "mp", ring)

    def both_cores(rows):
        return lax.all_gather(rows, "mp", axis=0, axis_index_groups=pairs)

    def opposite(block):
        half = lax.dynamic_slice_in_dim(block, lax.axis_index("mp") % 2, 1, 0)
        return hop(half)

    def projected(own, hop1, hop2):
        return call(
            functools.partial(partial_kernel, n_mp),
            (own, hop1, hop2, out_weight, pair_weight),
            (sds((2, own.shape[0], cols), F32), sds((2, cols, 3 * feat), BF16)),
            "partial",
        )

    def finished(acc, w_late, hop3, hop4):
        mine, pair = call(
            last_kernel, (acc, hop3, hop4, w_late), (sds((hop4.shape[1], cols), F32),) * 2, "last"
        )
        return mine, lax.ppermute(pair, "mp", swap)

    pos, og_moved = call(
        functools.partial(plan_kernel, n_dp),
        (destinations.reshape(1, tok), image_ids.reshape(1, tok), patch_counts.reshape(1, img), out_grad),
        (sds((8, tok), jnp.int32), sds((n_mp // 2, slots, feat), BF16)),
        "plan",
    )
    same_core = [list(range(core, n_mp, 2)) for core in range(2)]
    og_chips = lax.all_to_all(
        og_moved, "mp", split_axis=0, concat_axis=0, tiled=True, axis_index_groups=same_core
    )
    send, og_kept, rows_kept, used, kept_used, pos_col = call(
        functools.partial(pack_kernel, n_dp),
        (pos, out_grad, query_rows, key_rows, value_rows),
        (
            sds((exch, 3 * HD), BF16),
            sds((KEPT, feat), BF16),
            sds((KEPT, 3 * cols), BF16),
            sds((slots, HD), F32),
            sds((SMALL, HD), F32),
            sds((tok, HD), jnp.int32),
        ),
        "pack",
    )
    pair_weight = lax.ppermute(after(out_weight, pos), "mp", swap)
    kept_block = both_cores(og_kept)
    kept1 = hop(after(kept_block, og_chips))
    mine, pair = call(
        functools.partial(chips_kernel, n_mp),
        (og_chips, out_weight, pair_weight),
        (sds((slots, cols), F32),) * 2,
        "chips",
        24,
    )
    pair = lax.ppermute(pair, "mp", swap)
    moved_send = call(
        functools.partial(moved_kernel, n_dp),
        (mine, pair, send),
        sds((exch, 4 * HD), BF16),
        "moved",
        8,
    )
    rows_in = exchange(moved_send)
    kept2 = hop(after(kept1, moved_send))
    kept3 = hop(kept2)
    back_send = call(
        functools.partial(remote_kernel, n_dp, tok, img),
        (rows_in, used),
        sds((exch, 3 * HD), BF16),
        "remote",
        12,
    )
    back = exchange(back_send)
    kept4 = opposite(after(kept3, back_send))
    mine, pair = finished(*projected(og_kept, kept1, kept2), kept3, kept4)
    kept_grads = call(
        functools.partial(local_kernel, n_dp, tok, img),
        (mine, pair, rows_kept, kept_used, pos_col),
        (sds((tok, cols), BF16),) * 3,
        "kept",
        24,
    )
    return call(
        functools.partial(merge_kernel, n_dp),
        (back, pos_col) + kept_grads,
        (sds((tok, cols), BF16),) * 3,
        "merge",
        12,
    )


def solution(mesh):
    rows = P("dp", "mp")
    return jax.shard_map(
        local,
        mesh=mesh,
        in_specs=(rows, rows, rows, rows, P("mp", None), P("dp"), P("dp"), P("dp")),
        out_specs=(rows, rows, rows),
        check_vma=False,
    )
```

```python
import functools
import math

import jax
import jax.numpy as jnp
from jax import lax
from jax.experimental import pallas as pl
from jax.experimental.pallas import tpu as pltpu
from jax.sharding import PartitionSpec as P

HD = 128
CAP = 3
BIG = 256
SMALL = 144
KEPT = BIG + SMALL
OCT = 8
LOG2E = 1.4426950408889634
F32 = jnp.float32
BF16 = jnp.bfloat16
MIB = 1024 * 1024
NT = (((1,), (1,)), ((), ()))
TN = (((0,), (0,)), ((), ()))


def iota(shape, dim):
    return lax.broadcasted_iota(jnp.int32, shape, dim)


def one_hot(cond):
    return jnp.where(cond, 1.0, 0.0).astype(BF16)


def pick(hot, rows):
    return jnp.dot(hot, rows, preferred_element_type=F32).astype(BF16)


def slot_row(slot, n_dp):
    return OCT * (slot % n_dp) + 2 * (slot // n_dp)


def plan_kernel(n_dp, dest_ref, ids_ref, counts_ref, og_ref, pos_ref, og_moved_ref):
    tok = dest_ref.shape[1]
    slots = n_dp * CAP
    mine = lax.axis_index("dp")
    dest = dest_ref[...]
    counts = counts_ref[...]
    big_id = jnp.where(
        counts[:, 0:1] == BIG, 0, jnp.where(counts[:, 1:2] == BIG, 1, 2)
    )
    kept_class = jnp.where(ids_ref[...] == big_id, n_dp, n_dp + 1)
    group = jnp.where(dest == mine, kept_class, dest)
    n_rows = n_dp + 16
    row = iota((n_rows, tok), 0)
    member = row == group
    before = one_hot(iota((tok, tok), 0) < iota((tok, tok), 1))
    rank = jnp.dot(one_hot(member), before, preferred_element_type=F32)
    start = jnp.where(row < n_dp, row, jnp.where(row == n_dp, slots, slots + BIG))
    step = jnp.where(row < n_dp, float(n_dp), 1.0)
    place = jnp.where(member, start.astype(F32) + step * rank, 0.0)
    pos = jnp.sum(place, axis=0, keepdims=True).astype(jnp.int32)
    pos_ref[...] = jnp.broadcast_to(pos, pos_ref.shape)
    rows = pick(one_hot(iota((slots, tok), 0) == pos), og_ref[...])
    for copy in range(og_moved_ref.shape[0]):
        og_moved_ref[copy] = rows


def pack_kernel(
    n_dp, pos_ref, og_ref, q_ref, k_ref, v_ref,
    send_ref, og_kept_ref, rows_kept_ref, used_ref, kept_used_ref, pos_col_ref,
):
    tok = og_ref.shape[0]
    slots = n_dp * CAP
    pos = pos_ref[0:1, :]
    q, k, v = q_ref[...], k_ref[...], v_ref[...]
    first = jnp.where(pos < slots, slot_row(pos, n_dp), -OCT)
    row = iota((n_dp * OCT, tok), 0)
    left = jnp.concatenate([q, k[:, :HD]], 1)
    right = jnp.concatenate([k[:, HD:], v], 1)
    send_ref[...] = (
        jnp.dot(one_hot(row == first), left, preferred_element_type=F32)
        + jnp.dot(one_hot(row == first + 1), right, preferred_element_type=F32)
    ).astype(BF16)
    kept_hot = one_hot(iota((KEPT, tok), 0) + slots == pos)
    og_kept_ref[...] = pick(kept_hot, og_ref[...])
    rows_kept_ref[...] = pick(kept_hot, jnp.concatenate([q, k, v], 1))
    ones = jnp.ones((tok, HD), BF16)
    slot_hot = one_hot(iota((slots, tok), 0) == pos)
    used_ref[...] = jnp.dot(slot_hot, ones, preferred_element_type=F32)
    kept_used_ref[...] = jnp.dot(kept_hot[BIG:], ones, preferred_element_type=F32)
    wide = jnp.broadcast_to(pos.astype(F32), (HD, tok))
    pos_col_ref[...] = jnp.transpose(wide).astype(jnp.int32)


def attend(q, k, v, g, valid, weight):
    scale = 1.0 / HD**0.5
    scores = lax.dot_general(k, q, NT, preferred_element_type=F32)
    if valid is not None:
        scores = jnp.where(valid, scores, -1e30)
    top = jnp.max(scores, axis=0, keepdims=True)
    raised = jnp.exp2((scores - top) * (scale * LOG2E))
    total = jnp.sum(raised, axis=0, keepdims=True)
    probs = raised * (1.0 / total)
    prob_grad = lax.dot_general(v, g, NT, preferred_element_type=F32)
    row_dot = jnp.sum(probs * prob_grad, axis=0, keepdims=True)
    scaled = probs * weight
    value_grad = jnp.dot(scaled.astype(BF16), g, preferred_element_type=F32)
    score_grad = (scaled * (prob_grad - row_dot)).astype(BF16)
    key_grad = jnp.dot(score_grad, q, preferred_element_type=F32) * scale
    query_grad = lax.dot_general(score_grad, k, TN, preferred_element_type=F32) * scale
    return query_grad.astype(BF16), key_grad.astype(BF16), value_grad.astype(BF16)


def spread(n_dp, half, slots):
    shape = (n_dp * OCT, slots)
    return one_hot(iota(shape, 0) == slot_row(iota(shape, 1), n_dp) + half)


def moved_kernel(n_dp, own_ref, pair_ref, w_ref, rows_ref, send_ref):
    chips, slots, feat = own_ref.shape
    core = lax.axis_index("mp") % 2
    acc = jnp.zeros((slots, w_ref.shape[0]), F32)
    for chip in range(chips):
        for block_ref, parity in ((own_ref, core), (pair_ref, 1 - core)):
            start = pl.multiple_of((2 * chip + parity) * feat, HD)
            weight = w_ref[:, pl.ds(start, feat)]
            acc = acc + lax.dot_general(block_ref[chip], weight, NT, preferred_element_type=F32)
    grad = acc.astype(BF16)
    send_ref[:, : 3 * HD] = rows_ref[...]
    send_ref[:, 3 * HD :] = (
        jnp.dot(spread(n_dp, 0, slots), grad[:, :HD], preferred_element_type=F32)
        + jnp.dot(spread(n_dp, 1, slots), grad[:, HD:], preferred_element_type=F32)
    ).astype(BF16)


def remote_kernel(n_dp, tok, img, rows_ref, valid_ref, send_ref):
    slots = n_dp * CAP
    shape = (slots, n_dp * OCT)
    first = slot_row(iota(shape, 0), n_dp)
    hot0 = one_hot(iota(shape, 1) == first)
    hot1 = one_hot(iota(shape, 1) == first + 1)
    a, b = pick(hot0, rows_ref[...]), pick(hot1, rows_ref[...])
    valid = valid_ref[:, 0:1]
    count = jnp.sum(valid, axis=0, keepdims=True)
    weight = tok / (img * count)
    mask = valid > 0.5
    q0, q1, k0, g0 = (a[:, i * HD : (i + 1) * HD] for i in range(4))
    k1, v0, v1, g1 = (b[:, i * HD : (i + 1) * HD] for i in range(4))
    dq0, dk0, dv0 = attend(q0, k0, v0, g0, mask, weight)
    dq1, dk1, dv1 = attend(q1, k1, v1, g1, mask, weight)
    send_ref[...] = (
        jnp.dot(spread(n_dp, 0, slots), jnp.concatenate([dq0, dq1, dk0], 1), preferred_element_type=F32)
        + jnp.dot(spread(n_dp, 1, slots), jnp.concatenate([dk1, dv0, dv1], 1), preferred_element_type=F32)
    ).astype(BF16)


def project(og_ref, w_ref, acc_ref):
    blocks, _, cols = og_ref.shape

    @pl.when(pl.program_id(0) == 0)
    def _():
        acc_ref[...] = jnp.zeros_like(acc_ref)

    acc = acc_ref[...]
    for b in range(blocks):
        acc = acc + lax.dot_general(
            og_ref[b], w_ref[:, b * cols : (b + 1) * cols], NT, preferred_element_type=F32
        )
    acc_ref[...] = acc


def local_kernel(
    n_dp, tok, img, og_ref, w_ref, rows_ref, valid_ref, pos_ref,
    dq_ref, dk_ref, dv_ref, acc_ref,
):
    project(og_ref, w_ref, acc_ref)

    @pl.when(pl.program_id(0) == pl.num_programs(0) - 1)
    def _():
        slots = n_dp * CAP
        grad = acc_ref[...].astype(BF16)
        valid = valid_ref[:, 0:1]
        count = jnp.sum(valid, axis=0, keepdims=True)
        images = (
            (slice(0, BIG), None, tok / (img * BIG)),
            (slice(BIG, KEPT), valid > 0.5, tok / (img * count)),
        )
        parts = []
        for head in range(2):
            lanes = slice(head * HD, (head + 1) * HD)
            pieces = []
            for span, mask, weight in images:
                q = rows_ref[span, head * HD : (head + 1) * HD]
                k = rows_ref[span, (2 + head) * HD : (3 + head) * HD]
                v = rows_ref[span, (4 + head) * HD : (5 + head) * HD]
                pieces.append(attend(q, k, v, grad[span, lanes], mask, weight))
            parts.append([jnp.concatenate(p, 0) for p in zip(*pieces)])
        pos = pos_ref[:, 0:1] - slots
        hot = one_hot(iota((tok, KEPT), 1) == pos)
        for out, name in zip((dq_ref, dk_ref, dv_ref), range(3)):
            out[...] = pick(hot, jnp.concatenate([parts[0][name], parts[1][name]], 1))


def merge_kernel(n_dp, back_ref, pos_ref, q_ref, k_ref, v_ref, dq_ref, dk_ref, dv_ref):
    tok = q_ref.shape[0]
    slots = n_dp * CAP
    pos = pos_ref[:, 0:1]
    first = jnp.where(pos < slots, slot_row(pos, n_dp), -OCT)
    col = iota((tok, n_dp * OCT), 1)
    back = back_ref[...]
    a = pick(one_hot(col == first), back)
    b = pick(one_hot(col == first + 1), back)
    dq_ref[...] = q_ref[...] + a[:, : 2 * HD]
    dk_ref[...] = k_ref[...] + jnp.concatenate([a[:, 2 * HD :], b[:, :HD]], 1)
    dv_ref[...] = v_ref[...] + b[:, HD:]


def sds(shape, dtype):
    return jax.ShapeDtypeStruct(shape, dtype)


def call(kernel, ins, outs, name, vmem=56, flops=0):
    many = isinstance(outs, tuple)
    return pl.pallas_call(
        kernel,
        out_shape=outs,
        grid=(1,),
        in_specs=[whole(x) for x in ins],
        out_specs=tuple(whole(x) for x in outs) if many else whole(outs),
        **options(ins, outs if many else (outs,), name, vmem, flops),
    )(*ins)


def whole(x):
    zeros = (0,) * len(x.shape)
    return pl.BlockSpec(x.shape, lambda i: zeros)


def options(ins, outs, name, vmem, flops):
    size = sum(math.prod(x.shape) * x.dtype.itemsize for x in (*ins, *outs))
    return dict(
        compiler_params=pltpu.CompilerParams(vmem_limit_bytes=vmem * MIB),
        cost_estimate=pl.CostEstimate(flops=flops, bytes_accessed=size, transcendentals=0),
        name=name,
    )


def local(
    query_rows, key_rows, value_rows, out_grad, out_weight, destinations, image_ids, patch_counts
):
    tok, cols = query_rows.shape
    feat = out_grad.shape[1]
    n_dp, n_mp = lax.axis_size("dp"), lax.axis_size("mp")
    slots = n_dp * CAP
    img = patch_counts.shape[0]
    exch = n_dp * OCT
    swap = [(i, i ^ 1) for i in range(n_mp)]
    same_core = [list(range(core, n_mp, 2)) for core in range(2)]

    def exchange(rows):
        shaped = rows.reshape(n_dp, OCT, rows.shape[1])
        return lax.all_to_all(shaped, "dp", split_axis=0, concat_axis=0, tiled=True).reshape(rows.shape)

    def after(value, earlier):
        return lax.optimization_barrier((value, earlier))[0]

    pos, og_moved = call(
        functools.partial(plan_kernel, n_dp),
        (destinations.reshape(1, tok), image_ids.reshape(1, tok), patch_counts.reshape(1, img), out_grad),
        (sds((8, tok), jnp.int32), sds((n_mp // 2, slots, feat), BF16)),
        "plan",
    )
    og_chips = lax.all_to_all(
        og_moved, "mp", split_axis=0, concat_axis=0, tiled=True, axis_index_groups=same_core
    )
    og_pair = lax.ppermute(og_chips, "mp", swap)
    send, og_kept, rows_kept, used, kept_used, pos_col = call(
        functools.partial(pack_kernel, n_dp),
        (pos, out_grad, query_rows, key_rows, value_rows),
        (
            sds((exch, 3 * HD), BF16),
            sds((KEPT, feat), BF16),
            sds((KEPT, 3 * cols), BF16),
            sds((slots, HD), F32),
            sds((SMALL, HD), F32),
            sds((tok, HD), jnp.int32),
        ),
        "pack",
    )
    kept_all = lax.all_gather(after(og_kept, og_chips), "mp", axis=0)
    moved_send = call(
        functools.partial(moved_kernel, n_dp),
        (og_chips, og_pair, out_weight, send),
        sds((exch, 4 * HD), BF16),
        "moved",
        24,
    )
    rows_in = exchange(moved_send)
    back_send = call(
        functools.partial(remote_kernel, n_dp, tok, img),
        (rows_in, used),
        sds((exch, 3 * HD), BF16),
        "remote",
        12,
    )
    back = exchange(back_send)
    ins = (kept_all, out_weight, rows_kept, kept_used, pos_col)
    outs = (sds((tok, cols), BF16),) * 3
    per_step = 4 if n_mp % 4 == 0 else 1
    kept_grads = pl.pallas_call(
        functools.partial(local_kernel, n_dp, tok, img),
        out_shape=outs,
        grid=(n_mp // per_step,),
        in_specs=[
            pl.BlockSpec((per_step, KEPT, feat), lambda i: (i, 0, 0)),
            pl.BlockSpec((cols, per_step * feat), lambda i: (0, i)),
            *(whole(x) for x in ins[2:]),
        ],
        out_specs=tuple(whole(x) for x in outs),
        scratch_shapes=[pltpu.VMEM((KEPT, cols), F32)],
        **options(ins, outs, "kept", 56, 2 * KEPT * n_mp * feat * cols),
    )(*ins)
    return call(
        functools.partial(merge_kernel, n_dp),
        (back, pos_col) + kept_grads,
        (sds((tok, cols), BF16),) * 3,
        "merge",
        56,
    )


def solution(mesh):
    rows = P("dp", "mp")
    return jax.shard_map(
        local,
        mesh=mesh,
        in_specs=(rows, rows, rows, rows, P("mp", None), P("dp"), P("dp"), P("dp")),
        out_specs=(rows, rows, rows),
        check_vma=False,
    )
```

```python
import functools
import math

import jax
import jax.numpy as jnp
from jax import lax
from jax.experimental import pallas as pl
from jax.experimental.pallas import tpu as pltpu
from jax.sharding import PartitionSpec as P

HD = 128
CAP = 3
BIG = 256
SMALL = 144
KEPT = BIG + SMALL
OCT = 8
LOG2E = 1.4426950408889634
F32 = jnp.float32
BF16 = jnp.bfloat16
MIB = 1024 * 1024
NT = (((1,), (1,)), ((), ()))
TN = (((0,), (0,)), ((), ()))


def iota(shape, dim):
    return lax.broadcasted_iota(jnp.int32, shape, dim)


def one_hot(cond):
    return jnp.where(cond, 1.0, 0.0).astype(BF16)


def pick(hot, rows):
    return jnp.dot(hot, rows, preferred_element_type=F32).astype(BF16)


def to_octets(out_ref, wide_ref, first, blocks):
    slots = blocks[0].shape[0]
    for i, block in enumerate(blocks):
        wide_ref[pl.ds(first + i, slots, stride=OCT), :] = block.astype(F32)
    out_ref[...] = wide_ref[...].astype(BF16)


def from_octets(in_ref, wide_ref, count):
    wide_ref[...] = in_ref[...].astype(F32)
    slots = in_ref.shape[0] // OCT
    return [wide_ref[pl.ds(i, slots, stride=OCT), :].astype(BF16) for i in range(count)]


def plan_kernel(n_dp, dest_ref, ids_ref, counts_ref, og_ref, pos_ref, og_moved_ref):
    tok = dest_ref.shape[1]
    slots = n_dp * CAP
    mine = lax.axis_index("dp")
    dest = dest_ref[...]
    counts = counts_ref[...]
    big_id = jnp.where(
        counts[:, 0:1] == BIG, 0, jnp.where(counts[:, 1:2] == BIG, 1, 2)
    )
    kept_class = jnp.where(ids_ref[...] == big_id, n_dp, n_dp + 1)
    group = jnp.where(dest == mine, kept_class, dest)
    n_rows = n_dp + 16
    row = iota((n_rows, tok), 0)
    member = row == group
    before = one_hot(iota((tok, tok), 0) < iota((tok, tok), 1))
    rank = jnp.dot(one_hot(member), before, preferred_element_type=F32)
    start = jnp.where(row < n_dp, CAP * row, jnp.where(row == n_dp, slots, slots + BIG))
    place = jnp.where(member, start.astype(F32) + rank, 0.0)
    pos = jnp.sum(place, axis=0, keepdims=True).astype(jnp.int32)
    pos_ref[...] = jnp.broadcast_to(pos, pos_ref.shape)
    rows = pick(one_hot(iota((slots, tok), 0) == pos), og_ref[...])
    for copy in range(og_moved_ref.shape[0]):
        og_moved_ref[copy] = rows


def pack_kernel(
    n_dp, pos_ref, og_ref, q_ref, k_ref, v_ref,
    send_ref, og_kept_ref, rows_kept_ref, used_ref, kept_used_ref, pos_col_ref, wide_ref,
):
    tok = og_ref.shape[0]
    slots = n_dp * CAP
    pos = pos_ref[0:1, :]
    q, k, v = q_ref[...], k_ref[...], v_ref[...]
    rows = jnp.concatenate([q, k, v], 1)
    slot_hot = one_hot(iota((slots, tok), 0) == pos)
    sent = jnp.dot(slot_hot, rows, preferred_element_type=F32)
    wide_ref[...] = jnp.zeros_like(wide_ref)
    to_octets(send_ref, wide_ref, 0, [sent[:, i * HD : (i + 1) * HD] for i in range(6)])
    kept_hot = one_hot(iota((KEPT, tok), 0) + slots == pos)
    og_kept_ref[...] = pick(kept_hot, og_ref[...])
    rows_kept_ref[...] = pick(kept_hot, rows)
    ones = jnp.ones((tok, HD), BF16)
    used_ref[...] = jnp.dot(slot_hot, ones, preferred_element_type=F32)
    kept_used_ref[...] = jnp.dot(kept_hot[BIG:], ones, preferred_element_type=F32)
    wide = jnp.broadcast_to(pos.astype(F32), (HD, tok))
    pos_col_ref[...] = jnp.transpose(wide).astype(jnp.int32)


def attend(q, k, v, g, valid, weight):
    scale = 1.0 / HD**0.5
    scores = lax.dot_general(k, q, NT, preferred_element_type=F32)
    if valid is not None:
        scores = jnp.where(valid, scores, -1e30)
    top = jnp.max(scores, axis=0, keepdims=True)
    raised = jnp.exp2((scores - top) * (scale * LOG2E))
    total = jnp.sum(raised, axis=0, keepdims=True)
    probs = raised * (1.0 / total)
    prob_grad = lax.dot_general(v, g, NT, preferred_element_type=F32)
    row_dot = jnp.sum(probs * prob_grad, axis=0, keepdims=True)
    scaled = probs * weight
    value_grad = jnp.dot(scaled.astype(BF16), g, preferred_element_type=F32)
    score_grad = (scaled * (prob_grad - row_dot)).astype(BF16)
    key_grad = jnp.dot(score_grad, q, preferred_element_type=F32) * scale
    query_grad = lax.dot_general(score_grad, k, TN, preferred_element_type=F32) * scale
    return query_grad.astype(BF16), key_grad.astype(BF16), value_grad.astype(BF16)


def moved_kernel(own_ref, pair_ref, w_ref, rows_ref, send_ref, wide_ref):
    chips, slots, feat = own_ref.shape
    core = lax.axis_index("mp") % 2
    acc = jnp.zeros((slots, w_ref.shape[0]), F32)
    for chip in range(chips):
        for block_ref, parity in ((own_ref, core), (pair_ref, 1 - core)):
            start = pl.multiple_of((2 * chip + parity) * feat, HD)
            weight = w_ref[:, pl.ds(start, feat)]
            acc = acc + lax.dot_general(block_ref[chip], weight, NT, preferred_element_type=F32)
    grad = acc.astype(BF16)
    wide_ref[...] = rows_ref[...].astype(F32)
    to_octets(send_ref, wide_ref, 6, [grad[:, :HD], grad[:, HD:]])


def remote_kernel(tok, img, rows_ref, valid_ref, send_ref, wide_ref):
    q0, q1, k0, k1, v0, v1, g0, g1 = from_octets(rows_ref, wide_ref, OCT)
    valid = valid_ref[:, 0:1]
    count = jnp.sum(valid, axis=0, keepdims=True)
    weight = tok / (img * count)
    mask = valid > 0.5
    dq0, dk0, dv0 = attend(q0, k0, v0, g0, mask, weight)
    dq1, dk1, dv1 = attend(q1, k1, v1, g1, mask, weight)
    wide_ref[...] = jnp.zeros_like(wide_ref)
    to_octets(send_ref, wide_ref, 0, [dq0, dq1, dk0, dk1, dv0, dv1])


def project(og_ref, w_ref, acc_ref):
    blocks, _, cols = og_ref.shape

    @pl.when(pl.program_id(0) == 0)
    def _():
        acc_ref[...] = jnp.zeros_like(acc_ref)

    acc = acc_ref[...]
    for b in range(blocks):
        acc = acc + lax.dot_general(
            og_ref[b], w_ref[:, b * cols : (b + 1) * cols], NT, preferred_element_type=F32
        )
    acc_ref[...] = acc


def local_kernel(
    n_dp, tok, img, og_ref, w_ref, rows_ref, valid_ref, pos_ref,
    dq_ref, dk_ref, dv_ref, acc_ref,
):
    project(og_ref, w_ref, acc_ref)

    @pl.when(pl.program_id(0) == pl.num_programs(0) - 1)
    def _():
        slots = n_dp * CAP
        grad = acc_ref[...].astype(BF16)
        valid = valid_ref[:, 0:1]
        count = jnp.sum(valid, axis=0, keepdims=True)
        images = (
            (slice(0, BIG), None, tok / (img * BIG)),
            (slice(BIG, KEPT), valid > 0.5, tok / (img * count)),
        )
        parts = []
        for head in range(2):
            lanes = slice(head * HD, (head + 1) * HD)
            pieces = []
            for span, mask, weight in images:
                q = rows_ref[span, head * HD : (head + 1) * HD]
                k = rows_ref[span, (2 + head) * HD : (3 + head) * HD]
                v = rows_ref[span, (4 + head) * HD : (5 + head) * HD]
                pieces.append(attend(q, k, v, grad[span, lanes], mask, weight))
            parts.append([jnp.concatenate(p, 0) for p in zip(*pieces)])
        pos = pos_ref[:, 0:1] - slots
        hot = one_hot(iota((tok, KEPT), 1) == pos)
        for out, name in zip((dq_ref, dk_ref, dv_ref), range(3)):
            out[...] = pick(hot, jnp.concatenate([parts[0][name], parts[1][name]], 1))


def merge_kernel(back_ref, pos_ref, q_ref, k_ref, v_ref, dq_ref, dk_ref, dv_ref, wide_ref):
    tok = q_ref.shape[0]
    slots = back_ref.shape[0] // OCT
    hot = one_hot(iota((tok, slots), 1) == pos_ref[:, 0:1])
    back = from_octets(back_ref, wide_ref, 6)
    for i, (kept_ref, out) in enumerate(((q_ref, dq_ref), (k_ref, dk_ref), (v_ref, dv_ref))):
        rows = jnp.concatenate(back[2 * i : 2 * i + 2], 1)
        out[...] = kept_ref[...] + pick(hot, rows)


def sds(shape, dtype):
    return jax.ShapeDtypeStruct(shape, dtype)


def call(kernel, ins, outs, name, vmem=56, flops=0, scratch=()):
    many = isinstance(outs, tuple)
    return pl.pallas_call(
        kernel,
        out_shape=outs,
        grid=(1,),
        in_specs=[whole(x) for x in ins],
        out_specs=tuple(whole(x) for x in outs) if many else whole(outs),
        scratch_shapes=scratch,
        **options(ins, outs if many else (outs,), name, vmem, flops),
    )(*ins)


def whole(x):
    zeros = (0,) * len(x.shape)
    return pl.BlockSpec(x.shape, lambda i: zeros)


def options(ins, outs, name, vmem, flops):
    size = sum(math.prod(x.shape) * x.dtype.itemsize for x in (*ins, *outs))
    return dict(
        compiler_params=pltpu.CompilerParams(vmem_limit_bytes=vmem * MIB),
        cost_estimate=pl.CostEstimate(flops=flops, bytes_accessed=size, transcendentals=0),
        name=name,
    )


def local(
    query_rows, key_rows, value_rows, out_grad, out_weight, destinations, image_ids, patch_counts
):
    tok, cols = query_rows.shape
    feat = out_grad.shape[1]
    n_dp, n_mp = lax.axis_size("dp"), lax.axis_size("mp")
    slots = n_dp * CAP
    img = patch_counts.shape[0]
    exch = slots * OCT
    wide = [pltpu.VMEM((exch, HD), F32)]
    swap = [(i, i ^ 1) for i in range(n_mp)]
    same_core = [list(range(core, n_mp, 2)) for core in range(2)]

    def exchange(rows):
        shaped = rows.reshape(n_dp, CAP * OCT, HD)
        return lax.all_to_all(shaped, "dp", split_axis=0, concat_axis=0, tiled=True).reshape(rows.shape)

    def after(value, earlier):
        return lax.optimization_barrier((value, earlier))[0]

    pos, og_moved = call(
        functools.partial(plan_kernel, n_dp),
        (destinations.reshape(1, tok), image_ids.reshape(1, tok), patch_counts.reshape(1, img), out_grad),
        (sds((8, tok), jnp.int32), sds((n_mp // 2, slots, feat), BF16)),
        "plan",
    )
    og_chips = lax.all_to_all(
        og_moved, "mp", split_axis=0, concat_axis=0, tiled=True, axis_index_groups=same_core
    )
    og_pair = lax.ppermute(og_chips, "mp", swap)
    send, og_kept, rows_kept, used, kept_used, pos_col = call(
        functools.partial(pack_kernel, n_dp),
        (pos, out_grad, query_rows, key_rows, value_rows),
        (
            sds((exch, HD), BF16),
            sds((KEPT, feat), BF16),
            sds((KEPT, 3 * cols), BF16),
            sds((slots, HD), F32),
            sds((SMALL, HD), F32),
            sds((tok, HD), jnp.int32),
        ),
        "pack",
        scratch=wide,
    )
    kept_all = lax.all_gather(after(og_kept, og_chips), "mp", axis=0)
    moved_send = call(
        moved_kernel,
        (og_chips, og_pair, out_weight, send),
        sds((exch, HD), BF16),
        "moved",
        24,
        scratch=wide,
    )
    rows_in = exchange(moved_send)
    back_send = call(
        functools.partial(remote_kernel, tok, img),
        (rows_in, used),
        sds((exch, HD), BF16),
        "remote",
        12,
        scratch=wide,
    )
    back = exchange(back_send)
    ins = (kept_all, out_weight, rows_kept, kept_used, pos_col)
    outs = (sds((tok, cols), BF16),) * 3
    per_step = 4 if n_mp % 4 == 0 else 1
    kept_grads = pl.pallas_call(
        functools.partial(local_kernel, n_dp, tok, img),
        out_shape=outs,
        grid=(n_mp // per_step,),
        in_specs=[
            pl.BlockSpec((per_step, KEPT, feat), lambda i: (i, 0, 0)),
            pl.BlockSpec((cols, per_step * feat), lambda i: (0, i)),
            *(whole(x) for x in ins[2:]),
        ],
        out_specs=tuple(whole(x) for x in outs),
        scratch_shapes=[pltpu.VMEM((KEPT, cols), F32)],
        **options(ins, outs, "kept", 56, 2 * KEPT * n_mp * feat * cols),
    )(*ins)
    return call(
        merge_kernel,
        (back, pos_col) + kept_grads,
        (sds((tok, cols), BF16),) * 3,
        "merge",
        56,
        scratch=wide,
    )


def solution(mesh):
    rows = P("dp", "mp")
    return jax.shard_map(
        local,
        mesh=mesh,
        in_specs=(rows, rows, rows, rows, P("mp", None), P("dp"), P("dp"), P("dp")),
        out_specs=(rows, rows, rows),
        check_vma=False,
    )
```

```python
import functools
import math

import jax
import jax.numpy as jnp
from jax import lax
from jax.experimental import pallas as pl
from jax.experimental.pallas import tpu as pltpu
from jax.sharding import PartitionSpec as P

HD = 128
CAP = 3
BIG = 256
SMALL = 144
KEPT = BIG + SMALL
OCT = 8
LOG2E = 1.4426950408889634
CHUNKS = ((0, 208), (208, 192))
F32 = jnp.float32
BF16 = jnp.bfloat16
MIB = 1024 * 1024
NT = (((1,), (1,)), ((), ()))
TN = (((0,), (0,)), ((), ()))


def iota(shape, dim):
    return lax.broadcasted_iota(jnp.int32, shape, dim)


def one_hot(cond):
    return jnp.where(cond, 1.0, 0.0).astype(BF16)


def pick(hot, rows):
    return jnp.dot(hot, rows, preferred_element_type=F32).astype(BF16)


def to_octets(out_ref, wide_ref, first, blocks):
    slots = blocks[0].shape[0]
    for i, block in enumerate(blocks):
        wide_ref[pl.ds(first + i, slots, stride=OCT), :] = block.astype(F32)
    out_ref[...] = wide_ref[...].astype(BF16)


def from_octets(in_ref, wide_ref, count):
    wide_ref[...] = in_ref[...].astype(F32)
    slots = in_ref.shape[0] // OCT
    return [wide_ref[pl.ds(i, slots, stride=OCT), :].astype(BF16) for i in range(count)]


def plan_kernel(n_dp, dest_ref, ids_ref, counts_ref, og_ref, pos_ref, og_moved_ref):
    tok = dest_ref.shape[1]
    slots = n_dp * CAP
    mine = lax.axis_index("dp")
    dest = dest_ref[...]
    counts = counts_ref[...]
    big_id = jnp.where(
        counts[:, 0:1] == BIG, 0, jnp.where(counts[:, 1:2] == BIG, 1, 2)
    )
    kept_class = jnp.where(ids_ref[...] == big_id, n_dp, n_dp + 1)
    group = jnp.where(dest == mine, kept_class, dest)
    n_rows = n_dp + 16
    row = iota((n_rows, tok), 0)
    member = row == group
    before = one_hot(iota((tok, tok), 0) < iota((tok, tok), 1))
    rank = jnp.dot(one_hot(member), before, preferred_element_type=F32)
    start = jnp.where(row < n_dp, CAP * row, jnp.where(row == n_dp, slots, slots + BIG))
    place = jnp.where(member, start.astype(F32) + rank, 0.0)
    pos = jnp.sum(place, axis=0, keepdims=True).astype(jnp.int32)
    pos_ref[...] = jnp.broadcast_to(pos, pos_ref.shape)
    rows = pick(one_hot(iota((slots, tok), 0) == pos), og_ref[...])
    for copy in range(og_moved_ref.shape[0]):
        og_moved_ref[copy] = rows


def pack_kernel(
    n_dp, pos_ref, og_ref, q_ref, k_ref, v_ref,
    send_ref, og_kept_ref, rows_kept_ref, used_ref, kept_used_ref, pos_col_ref, wide_ref,
):
    tok = og_ref.shape[0]
    slots = n_dp * CAP
    pos = pos_ref[0:1, :]
    q, k, v = q_ref[...], k_ref[...], v_ref[...]
    rows = jnp.concatenate([q, k, v], 1)
    slot_hot = one_hot(iota((slots, tok), 0) == pos)
    sent = jnp.dot(slot_hot, rows, preferred_element_type=F32)
    wide_ref[...] = jnp.zeros_like(wide_ref)
    to_octets(send_ref, wide_ref, 0, [sent[:, i * HD : (i + 1) * HD] for i in range(6)])
    kept_hot = one_hot(iota((KEPT, tok), 0) + slots == pos)
    og_kept_ref[...] = pick(kept_hot, og_ref[...])
    rows_kept_ref[...] = pick(kept_hot, rows)
    ones = jnp.ones((tok, HD), BF16)
    used_ref[...] = jnp.dot(slot_hot, ones, preferred_element_type=F32)
    kept_used_ref[...] = jnp.dot(kept_hot[BIG:], ones, preferred_element_type=F32)
    wide = jnp.broadcast_to(pos.astype(F32), (HD, tok))
    pos_col_ref[...] = jnp.transpose(wide).astype(jnp.int32)


def attend(q, k, v, g, valid, weight):
    scale = 1.0 / HD**0.5
    scores = lax.dot_general(k, q, NT, preferred_element_type=F32)
    if valid is not None:
        scores = jnp.where(valid, scores, -1e30)
    top = jnp.max(scores, axis=0, keepdims=True)
    raised = jnp.exp2((scores - top) * (scale * LOG2E))
    total = jnp.sum(raised, axis=0, keepdims=True)
    probs = raised * (1.0 / total)
    prob_grad = lax.dot_general(v, g, NT, preferred_element_type=F32)
    row_dot = jnp.sum(probs * prob_grad, axis=0, keepdims=True)
    scaled = probs * weight
    value_grad = jnp.dot(scaled.astype(BF16), g, preferred_element_type=F32)
    score_grad = (scaled * (prob_grad - row_dot)).astype(BF16)
    key_grad = jnp.dot(score_grad, q, preferred_element_type=F32) * scale
    query_grad = lax.dot_general(score_grad, k, TN, preferred_element_type=F32) * scale
    return query_grad.astype(BF16), key_grad.astype(BF16), value_grad.astype(BF16)


def block_dot(rows, w_ref, start):
    cols = rows.shape[1]
    weight = w_ref[:, pl.ds(pl.multiple_of(start, HD), cols)]
    return lax.dot_general(rows, weight, NT, preferred_element_type=F32)


def source_start(n_mp, me, away, feat):
    chips = n_mp // 2
    chip, core = me // 2, me % 2
    return (jnp.where(core == 0, chip - away, chip + away) + chips) % chips * (2 * feat)


def partial_kernel(n_mp, own_ref, *refs):
    *hop_refs, w_ref, w_pair_ref, acc_ref, w_late_ref = refs
    chunks = len(hop_refs) // 2
    feat = own_ref.shape[1]
    me = lax.axis_index("mp")
    third = pl.multiple_of(source_start(n_mp, me, 3, feat), HD)
    last = pl.multiple_of((me + n_mp // 2) % n_mp * feat, HD)
    for side, weight_ref in enumerate((w_ref, w_pair_ref)):
        row = 0
        for chunk in range(chunks):
            rows = hop_refs[chunk].shape[1]
            acc = block_dot(own_ref[row : row + rows], weight_ref, me * feat)
            for hop in range(2):
                block_ref = hop_refs[hop * chunks + chunk]
                start = source_start(n_mp, me, hop + 1, feat)
                for half in range(2):
                    acc = acc + block_dot(block_ref[half], weight_ref, start + half * feat)
            acc_ref[side, row : row + rows] = acc
            row += rows
        w_late_ref[side, :, : 2 * feat] = weight_ref[:, pl.ds(third, 2 * feat)]
        w_late_ref[side, :, 2 * feat :] = weight_ref[:, pl.ds(last, feat)]


def last_kernel(acc_ref, *refs):
    *hop_refs, w_late_ref, mine_ref, pair_ref = refs
    chunks = len(hop_refs) // 2
    feat = hop_refs[0].shape[2]
    for side, out in enumerate((mine_ref, pair_ref)):
        row = 0
        for chunk in range(chunks):
            hop3_ref, hop4_ref = hop_refs[chunk], hop_refs[chunks + chunk]
            rows = hop3_ref.shape[1]
            acc = acc_ref[side, row : row + rows]
            for part, block in enumerate((hop3_ref[0], hop3_ref[1], hop4_ref[0])):
                weight = w_late_ref[side, :, part * feat : (part + 1) * feat]
                acc = acc + lax.dot_general(block, weight, NT, preferred_element_type=F32)
            out[row : row + rows] = acc
            row += rows


def chips_kernel(n_mp, og_ref, w_ref, w_pair_ref, mine_ref, pair_ref):
    chips, _, feat = og_ref.shape
    core = lax.axis_index("mp") % 2
    for weight_ref, out in ((w_ref, mine_ref), (w_pair_ref, pair_ref)):
        acc = block_dot(og_ref[0], weight_ref, core * feat)
        for chip in range(1, chips):
            acc = acc + block_dot(og_ref[chip], weight_ref, (2 * chip + core) * feat)
        out[...] = acc


def moved_kernel(mine_ref, pair_ref, rows_ref, send_ref, wide_ref):
    grad = mine_ref[...] + pair_ref[...]
    wide_ref[...] = rows_ref[...].astype(F32)
    to_octets(send_ref, wide_ref, 6, [grad[:, :HD], grad[:, HD:]])


def remote_kernel(tok, img, rows_ref, valid_ref, send_ref, wide_ref):
    q0, q1, k0, k1, v0, v1, g0, g1 = from_octets(rows_ref, wide_ref, OCT)
    valid = valid_ref[:, 0:1]
    count = jnp.sum(valid, axis=0, keepdims=True)
    weight = tok / (img * count)
    mask = valid > 0.5
    dq0, dk0, dv0 = attend(q0, k0, v0, g0, mask, weight)
    dq1, dk1, dv1 = attend(q1, k1, v1, g1, mask, weight)
    wide_ref[...] = jnp.zeros_like(wide_ref)
    to_octets(send_ref, wide_ref, 0, [dq0, dq1, dk0, dk1, dv0, dv1])


def local_kernel(
    n_dp, tok, img, mine_ref, pair_ref, rows_ref, valid_ref, pos_ref, dq_ref, dk_ref, dv_ref
):
    slots = n_dp * CAP
    grad = (mine_ref[...] + pair_ref[...]).astype(BF16)
    valid = valid_ref[:, 0:1]
    count = jnp.sum(valid, axis=0, keepdims=True)
    images = (
        (slice(0, BIG), None, tok / (img * BIG)),
        (slice(BIG, KEPT), valid > 0.5, tok / (img * count)),
    )
    parts = []
    for head in range(2):
        lanes = slice(head * HD, (head + 1) * HD)
        pieces = []
        for span, mask, weight in images:
            q = rows_ref[span, head * HD : (head + 1) * HD]
            k = rows_ref[span, (2 + head) * HD : (3 + head) * HD]
            v = rows_ref[span, (4 + head) * HD : (5 + head) * HD]
            pieces.append(attend(q, k, v, grad[span, lanes], mask, weight))
        parts.append([jnp.concatenate(p, 0) for p in zip(*pieces)])
    pos = pos_ref[:, 0:1] - slots
    hot = one_hot(iota((tok, KEPT), 1) == pos)
    for name, out in enumerate((dq_ref, dk_ref, dv_ref)):
        out[...] = pick(hot, jnp.concatenate([parts[0][name], parts[1][name]], 1))


def merge_kernel(back_ref, pos_ref, q_ref, k_ref, v_ref, dq_ref, dk_ref, dv_ref, wide_ref):
    tok = q_ref.shape[0]
    slots = back_ref.shape[0] // OCT
    hot = one_hot(iota((tok, slots), 1) == pos_ref[:, 0:1])
    back = from_octets(back_ref, wide_ref, 6)
    for i, (kept_ref, out) in enumerate(((q_ref, dq_ref), (k_ref, dk_ref), (v_ref, dv_ref))):
        rows = jnp.concatenate(back[2 * i : 2 * i + 2], 1)
        out[...] = kept_ref[...] + pick(hot, rows)


def sds(shape, dtype):
    return jax.ShapeDtypeStruct(shape, dtype)


def call(kernel, ins, outs, name, vmem=56, flops=0, scratch=()):
    many = isinstance(outs, tuple)
    return pl.pallas_call(
        kernel,
        out_shape=outs,
        grid=(1,),
        in_specs=[whole(x) for x in ins],
        out_specs=tuple(whole(x) for x in outs) if many else whole(outs),
        scratch_shapes=scratch,
        **options(ins, outs if many else (outs,), name, vmem, flops),
    )(*ins)


def whole(x):
    zeros = (0,) * len(x.shape)
    return pl.BlockSpec(x.shape, lambda i: zeros)


def options(ins, outs, name, vmem, flops):
    size = sum(math.prod(x.shape) * x.dtype.itemsize for x in (*ins, *outs))
    return dict(
        compiler_params=pltpu.CompilerParams(vmem_limit_bytes=vmem * MIB),
        cost_estimate=pl.CostEstimate(flops=flops, bytes_accessed=size, transcendentals=0),
        name=name,
    )


def local(
    query_rows, key_rows, value_rows, out_grad, out_weight, destinations, image_ids, patch_counts
):
    tok, cols = query_rows.shape
    feat = out_grad.shape[1]
    n_dp, n_mp = lax.axis_size("dp"), lax.axis_size("mp")
    slots = n_dp * CAP
    img = patch_counts.shape[0]
    exch = slots * OCT
    wide = [pltpu.VMEM((exch, HD), F32)]
    swap = [(i, i ^ 1) for i in range(n_mp)]
    pairs = [[2 * i, 2 * i + 1] for i in range(n_mp // 2)]
    ring = [(i, (i + (2 if i % 2 == 0 else -2)) % n_mp) for i in range(n_mp)]
    same_core = [list(range(core, n_mp, 2)) for core in range(2)]

    def exchange(rows):
        shaped = rows.reshape(n_dp, CAP * OCT, HD)
        return lax.all_to_all(shaped, "dp", split_axis=0, concat_axis=0, tiled=True).reshape(rows.shape)

    def after(value, earlier):
        return lax.optimization_barrier((value, earlier))[0]

    def hop(block):
        return lax.ppermute(block, "mp", ring)

    def opposite(block):
        return hop(lax.dynamic_slice_in_dim(block, lax.axis_index("mp") % 2, 1, 0))

    def in_chunks(block):
        return [block[:, start : start + size] for start, size in CHUNKS]

    pair_weight = lax.ppermute(out_weight, "mp", swap)
    pos, og_moved = call(
        functools.partial(plan_kernel, n_dp),
        (destinations.reshape(1, tok), image_ids.reshape(1, tok), patch_counts.reshape(1, img), out_grad),
        (sds((8, tok), jnp.int32), sds((n_mp // 2, slots, feat), BF16)),
        "plan",
    )
    og_chips = lax.all_to_all(
        og_moved, "mp", split_axis=0, concat_axis=0, tiled=True, axis_index_groups=same_core
    )
    send, og_kept, rows_kept, used, kept_used, pos_col = call(
        functools.partial(pack_kernel, n_dp),
        (pos, out_grad, query_rows, key_rows, value_rows),
        (
            sds((exch, HD), BF16),
            sds((KEPT, feat), BF16),
            sds((KEPT, 3 * cols), BF16),
            sds((slots, HD), F32),
            sds((SMALL, HD), F32),
            sds((tok, HD), jnp.int32),
        ),
        "pack",
        scratch=wide,
    )
    kept_block = lax.all_gather(og_kept, "mp", axis=0, axis_index_groups=pairs)
    og_chips = after(og_chips, kept_block)
    kept_blocks = in_chunks(kept_block)
    mine, pair = call(
        functools.partial(chips_kernel, n_mp),
        (og_chips, out_weight, pair_weight),
        (sds((slots, cols), F32),) * 2,
        "chips",
        24,
    )
    pair = lax.ppermute(pair, "mp", swap)
    kept1 = [hop(after(x, mine)) for x in kept_blocks]
    moved_send = call(
        moved_kernel,
        (mine, pair, send),
        sds((exch, HD), BF16),
        "moved",
        8,
        scratch=wide,
    )
    rows_in = exchange(moved_send)
    kept2 = [hop(after(x, moved_send)) for x in kept1]
    kept3 = [hop(x) for x in kept2]
    back_send = call(
        functools.partial(remote_kernel, tok, img),
        (rows_in, used),
        sds((exch, HD), BF16),
        "remote",
        12,
        scratch=wide,
    )
    back = exchange(back_send)
    kept4 = [opposite(x) for x in kept3]
    acc, w_late = call(
        functools.partial(partial_kernel, n_mp),
        (og_kept, *kept1, *kept2, out_weight, pair_weight),
        (sds((2, KEPT, cols), F32), sds((2, cols, 3 * feat), BF16)),
        "partial",
        56,
        2 * KEPT * n_mp * feat * cols,
    )
    mine, pair = call(
        last_kernel, (acc, *kept3, *kept4, w_late), (sds((KEPT, cols), F32),) * 2, "last"
    )
    pair = lax.ppermute(pair, "mp", swap)
    kept_grads = call(
        functools.partial(local_kernel, n_dp, tok, img),
        (mine, pair, rows_kept, kept_used, pos_col),
        (sds((tok, cols), BF16),) * 3,
        "kept",
        24,
    )
    return call(
        merge_kernel,
        (back, pos_col) + kept_grads,
        (sds((tok, cols), BF16),) * 3,
        "merge",
        12,
        scratch=wide,
    )


def solution(mesh):
    rows = P("dp", "mp")
    return jax.shard_map(
        local,
        mesh=mesh,
        in_specs=(rows, rows, rows, rows, P("mp", None), P("dp"), P("dp"), P("dp")),
        out_specs=(rows, rows, rows),
        check_vma=False,
    )
```

```python
import functools
import math

import jax
import jax.numpy as jnp
from jax import lax
from jax.experimental import pallas as pl
from jax.experimental.pallas import tpu as pltpu
from jax.sharding import PartitionSpec as P

HD = 128
CAP = 3
BIG = 256
SMALL = 144
KEPT = BIG + SMALL
OCT = 8
LOG2E = 1.4426950408889634
F32 = jnp.float32
BF16 = jnp.bfloat16
MIB = 1024 * 1024
NT = (((1,), (1,)), ((), ()))
TN = (((0,), (0,)), ((), ()))


def iota(shape, dim):
    return lax.broadcasted_iota(jnp.int32, shape, dim)


def one_hot(cond):
    return jnp.where(cond, 1.0, 0.0).astype(BF16)


def pick(hot, rows):
    return jnp.dot(hot, rows, preferred_element_type=F32).astype(BF16)


def to_octets(out_ref, wide_ref, first, blocks):
    slots = blocks[0].shape[0]
    for i, block in enumerate(blocks):
        wide_ref[pl.ds(first + i, slots, stride=OCT), :] = block.astype(F32)
    out_ref[...] = wide_ref[...].astype(BF16)


def from_octets(in_ref, wide_ref, count):
    wide_ref[...] = in_ref[...].astype(F32)
    slots = in_ref.shape[0] // OCT
    return [wide_ref[pl.ds(i, slots, stride=OCT), :].astype(BF16) for i in range(count)]


def plan_kernel(n_dp, dest_ref, ids_ref, counts_ref, og_ref, pos_ref, og_moved_ref):
    tok = dest_ref.shape[1]
    slots = n_dp * CAP
    mine = lax.axis_index("dp")
    dest = dest_ref[...]
    counts = counts_ref[...]
    big_id = jnp.where(
        counts[:, 0:1] == BIG, 0, jnp.where(counts[:, 1:2] == BIG, 1, 2)
    )
    kept_class = jnp.where(ids_ref[...] == big_id, n_dp, n_dp + 1)
    group = jnp.where(dest == mine, kept_class, dest)
    n_rows = n_dp + 16
    row = iota((n_rows, tok), 0)
    member = row == group
    before = one_hot(iota((tok, tok), 0) < iota((tok, tok), 1))
    rank = jnp.dot(one_hot(member), before, preferred_element_type=F32)
    start = jnp.where(row < n_dp, CAP * row, jnp.where(row == n_dp, slots, slots + BIG))
    place = jnp.where(member, start.astype(F32) + rank, 0.0)
    pos = jnp.sum(place, axis=0, keepdims=True).astype(jnp.int32)
    pos_ref[...] = jnp.broadcast_to(pos, pos_ref.shape)
    rows = pick(one_hot(iota((slots, tok), 0) == pos), og_ref[...])
    for copy in range(og_moved_ref.shape[0]):
        og_moved_ref[copy] = rows


def pack_kernel(
    n_dp, pos_ref, og_ref, q_ref, k_ref, v_ref,
    send_ref, og_kept_ref, rows_kept_ref, used_ref, kept_used_ref, pos_col_ref, wide_ref,
):
    tok = og_ref.shape[0]
    slots = n_dp * CAP
    pos = pos_ref[0:1, :]
    q, k, v = q_ref[...], k_ref[...], v_ref[...]
    rows = jnp.concatenate([q, k, v], 1)
    slot_hot = one_hot(iota((slots, tok), 0) == pos)
    sent = jnp.dot(slot_hot, rows, preferred_element_type=F32)
    wide_ref[...] = jnp.zeros_like(wide_ref)
    to_octets(send_ref, wide_ref, 0, [sent[:, i * HD : (i + 1) * HD] for i in range(6)])
    kept_hot = one_hot(iota((KEPT, tok), 0) + slots == pos)
    og_kept_ref[...] = pick(kept_hot, og_ref[...])
    rows_kept_ref[...] = pick(kept_hot, rows)
    ones = jnp.ones((tok, HD), BF16)
    used_ref[...] = jnp.dot(slot_hot, ones, preferred_element_type=F32)
    kept_used_ref[...] = jnp.dot(kept_hot[BIG:], ones, preferred_element_type=F32)
    wide = jnp.broadcast_to(pos.astype(F32), (HD, tok))
    pos_col_ref[...] = jnp.transpose(wide).astype(jnp.int32)


def attend(q, k, v, g, valid, weight):
    scale = 1.0 / HD**0.5
    scores = lax.dot_general(k, q, NT, preferred_element_type=F32)
    if valid is not None:
        scores = jnp.where(valid, scores, -1e30)
    top = jnp.max(scores, axis=0, keepdims=True)
    raised = jnp.exp2((scores - top) * (scale * LOG2E))
    total = jnp.sum(raised, axis=0, keepdims=True)
    probs = raised * (1.0 / total)
    prob_grad = lax.dot_general(v, g, NT, preferred_element_type=F32)
    row_dot = jnp.sum(probs * prob_grad, axis=0, keepdims=True)
    scaled = probs * weight
    value_grad = jnp.dot(scaled.astype(BF16), g, preferred_element_type=F32)
    score_grad = (scaled * (prob_grad - row_dot)).astype(BF16)
    key_grad = jnp.dot(score_grad, q, preferred_element_type=F32) * scale
    query_grad = lax.dot_general(score_grad, k, TN, preferred_element_type=F32) * scale
    return query_grad.astype(BF16), key_grad.astype(BF16), value_grad.astype(BF16)


def parity_dot(block_ref, w_ref, parity):
    chips, rows, feat = block_ref.shape
    acc = jnp.zeros((rows, w_ref.shape[0]), F32)
    for chip in range(chips):
        start = pl.multiple_of((2 * chip + parity) * feat, HD)
        weight = w_ref[:, pl.ds(start, feat)]
        acc = acc + lax.dot_general(block_ref[chip], weight, NT, preferred_element_type=F32)
    return acc


def own_kernel(own_ref, w_ref, acc_ref):
    acc_ref[...] = parity_dot(own_ref, w_ref, lax.axis_index("mp") % 2)


def moved_kernel(acc_ref, pair_ref, w_ref, rows_hbm, send_ref, wide_ref, rows_ref, sem):
    fetch = pltpu.make_async_copy(rows_hbm, rows_ref, sem)
    fetch.start()
    grad = acc_ref[...] + parity_dot(pair_ref, w_ref, 1 - lax.axis_index("mp") % 2)
    fetch.wait()
    wide_ref[...] = rows_ref[...].astype(F32)
    to_octets(send_ref, wide_ref, 6, [grad[:, :HD], grad[:, HD:]])


def remote_kernel(tok, img, rows_ref, valid_ref, send_ref, wide_ref):
    q0, q1, k0, k1, v0, v1, g0, g1 = from_octets(rows_ref, wide_ref, OCT)
    valid = valid_ref[:, 0:1]
    count = jnp.sum(valid, axis=0, keepdims=True)
    weight = tok / (img * count)
    mask = valid > 0.5
    dq0, dk0, dv0 = attend(q0, k0, v0, g0, mask, weight)
    dq1, dk1, dv1 = attend(q1, k1, v1, g1, mask, weight)
    wide_ref[...] = jnp.zeros_like(wide_ref)
    to_octets(send_ref, wide_ref, 0, [dq0, dq1, dk0, dk1, dv0, dv1])


def project(og_ref, w_ref, acc_ref):
    blocks, _, cols = og_ref.shape

    @pl.when(pl.program_id(0) == 0)
    def _():
        acc_ref[...] = jnp.zeros_like(acc_ref)

    acc = acc_ref[...]
    for b in range(0, blocks, 2):
        rows = jnp.concatenate([og_ref[i] for i in range(b, min(b + 2, blocks))], 1)
        weight = w_ref[:, b * cols : b * cols + rows.shape[1]]
        acc = acc + lax.dot_general(rows, weight, NT, preferred_element_type=F32)
    acc_ref[...] = acc


def local_kernel(
    n_dp, tok, img, og_ref, w_ref, rows_ref, valid_ref, pos_ref,
    grads_ref, acc_ref,
):
    project(og_ref, w_ref, acc_ref)

    @pl.when(pl.program_id(0) == pl.num_programs(0) - 1)
    def _():
        slots = n_dp * CAP
        grad = acc_ref[...].astype(BF16)
        valid = valid_ref[:, 0:1]
        count = jnp.sum(valid, axis=0, keepdims=True)
        images = (
            (slice(0, BIG), None, tok / (img * BIG)),
            (slice(BIG, KEPT), valid > 0.5, tok / (img * count)),
        )
        parts = []
        for head in range(2):
            lanes = slice(head * HD, (head + 1) * HD)
            pieces = []
            for span, mask, weight in images:
                q = rows_ref[span, head * HD : (head + 1) * HD]
                k = rows_ref[span, (2 + head) * HD : (3 + head) * HD]
                v = rows_ref[span, (4 + head) * HD : (5 + head) * HD]
                pieces.append(attend(q, k, v, grad[span, lanes], mask, weight))
            parts.append([jnp.concatenate(p, 0) for p in zip(*pieces)])
        pos = pos_ref[:, 0:1] - slots
        hot = one_hot(iota((tok, KEPT), 1) == pos)
        for name in range(3):
            grads_ref[name] = pick(hot, jnp.concatenate([parts[0][name], parts[1][name]], 1))


def merge_kernel(back_ref, pos_hbm, kept_hbm, dq_ref, dk_ref, dv_ref, wide_ref, pos_ref, kept_ref, sems):
    fetches = [
        pltpu.make_async_copy(pos_hbm, pos_ref, sems.at[0]),
        pltpu.make_async_copy(kept_hbm, kept_ref, sems.at[1]),
    ]
    for fetch in fetches:
        fetch.start()
    back = from_octets(back_ref, wide_ref, 6)
    fetches[0].wait()
    slots = back_ref.shape[0] // OCT
    hot = one_hot(iota((pos_ref.shape[0], slots), 1) == pos_ref[:, 0:1])
    added = [pick(hot, jnp.concatenate(back[2 * i : 2 * i + 2], 1)) for i in range(3)]
    fetches[1].wait()
    for i, out in enumerate((dq_ref, dk_ref, dv_ref)):
        out[...] = kept_ref[i] + added[i]


def sds(shape, dtype):
    return jax.ShapeDtypeStruct(shape, dtype)


def call(kernel, ins, outs, name, vmem=56, flops=0, scratch=(), in_hbm=()):
    many = isinstance(outs, tuple)
    return pl.pallas_call(
        kernel,
        out_shape=outs,
        grid=(1,),
        in_specs=[
            pl.BlockSpec(memory_space=pltpu.HBM) if i in in_hbm else whole(x)
            for i, x in enumerate(ins)
        ],
        out_specs=tuple(whole(x) for x in outs) if many else whole(outs),
        scratch_shapes=scratch,
        **options(ins, outs if many else (outs,), name, vmem, flops),
    )(*ins)


def whole(x):
    zeros = (0,) * len(x.shape)
    return pl.BlockSpec(x.shape, lambda i: zeros)


def options(ins, outs, name, vmem, flops):
    size = sum(math.prod(x.shape) * x.dtype.itemsize for x in (*ins, *outs))
    return dict(
        compiler_params=pltpu.CompilerParams(vmem_limit_bytes=vmem * MIB),
        cost_estimate=pl.CostEstimate(flops=flops, bytes_accessed=size, transcendentals=0),
        name=name,
    )


def local(
    query_rows, key_rows, value_rows, out_grad, out_weight, destinations, image_ids, patch_counts
):
    tok, cols = query_rows.shape
    feat = out_grad.shape[1]
    n_dp, n_mp = lax.axis_size("dp"), lax.axis_size("mp")
    slots = n_dp * CAP
    img = patch_counts.shape[0]
    exch = slots * OCT
    wide = [pltpu.VMEM((exch, HD), F32)]
    swap = [(i, i ^ 1) for i in range(n_mp)]
    same_core = [list(range(core, n_mp, 2)) for core in range(2)]

    def exchange(rows):
        shaped = rows.reshape(n_dp, CAP * OCT, HD)
        return lax.all_to_all(shaped, "dp", split_axis=0, concat_axis=0, tiled=True).reshape(rows.shape)

    def after(value, earlier):
        return lax.optimization_barrier((value, earlier))[0]

    pos, og_moved = call(
        functools.partial(plan_kernel, n_dp),
        (destinations.reshape(1, tok), image_ids.reshape(1, tok), patch_counts.reshape(1, img), out_grad),
        (sds((8, tok), jnp.int32), sds((n_mp // 2, slots, feat), BF16)),
        "plan",
    )
    og_chips = lax.all_to_all(
        og_moved, "mp", split_axis=0, concat_axis=0, tiled=True, axis_index_groups=same_core
    )
    og_pair = lax.ppermute(og_chips, "mp", swap)
    send, og_kept, rows_kept, used, kept_used, pos_col = call(
        functools.partial(pack_kernel, n_dp),
        (pos, out_grad, query_rows, key_rows, value_rows),
        (
            sds((exch, HD), BF16),
            sds((KEPT, feat), BF16),
            sds((KEPT, 3 * cols), BF16),
            sds((slots, HD), F32),
            sds((SMALL, HD), F32),
            sds((tok, HD), jnp.int32),
        ),
        "pack",
        scratch=wide,
    )
    kept_all = lax.all_gather(after(og_kept, og_chips), "mp", axis=0)
    own = call(
        own_kernel, (og_chips, out_weight), sds((slots, cols), F32), "own", 24, 10**9
    )
    moved_send = call(
        moved_kernel,
        (own, og_pair, out_weight, send),
        sds((exch, HD), BF16),
        "moved",
        24,
        scratch=wide + [pltpu.VMEM((exch, HD), BF16), pltpu.SemaphoreType.DMA],
        in_hbm=(3,),
    )
    rows_in = exchange(moved_send)
    back_send = call(
        functools.partial(remote_kernel, tok, img),
        (rows_in, used),
        sds((exch, HD), BF16),
        "remote",
        12,
        scratch=wide,
    )
    back = exchange(back_send)
    ins = (kept_all, out_weight, rows_kept, kept_used, pos_col)
    outs = sds((3, tok, cols), BF16)
    per_step = 4 if n_mp % 4 == 0 else 1
    kept_grads = pl.pallas_call(
        functools.partial(local_kernel, n_dp, tok, img),
        out_shape=outs,
        grid=(n_mp // per_step,),
        in_specs=[
            pl.BlockSpec((per_step, KEPT, feat), lambda i: (i, 0, 0)),
            pl.BlockSpec((cols, per_step * feat), lambda i: (0, i)),
            *(whole(x) for x in ins[2:]),
        ],
        out_specs=whole(outs),
        scratch_shapes=[pltpu.VMEM((KEPT, cols), F32)],
        **options(ins, (outs,), "kept", 56, 2 * KEPT * n_mp * feat * cols),
    )(*ins)
    return call(
        merge_kernel,
        (back, pos_col, kept_grads),
        (sds((tok, cols), BF16),) * 3,
        "merge",
        56,
        scratch=wide
        + [
            pltpu.VMEM((tok, HD), jnp.int32),
            pltpu.VMEM((3, tok, cols), BF16),
            pltpu.SemaphoreType.DMA((2,)),
        ],
        in_hbm=(1, 2),
    )


def solution(mesh):
    rows = P("dp", "mp")
    return jax.shard_map(
        local,
        mesh=mesh,
        in_specs=(rows, rows, rows, rows, P("mp", None), P("dp"), P("dp"), P("dp")),
        out_specs=(rows, rows, rows),
        check_vma=False,
    )
```

```python
import functools
import math

import jax
import jax.numpy as jnp
from jax import lax
from jax.experimental import pallas as pl
from jax.experimental.pallas import tpu as pltpu
from jax.sharding import PartitionSpec as P

HD = 128
CAP = 3
BIG = 256
SMALL = 144
KEPT = BIG + SMALL
OCT = 8
LOG2E = 1.4426950408889634
CHUNKS = ((0, 208), (208, 192))
F32 = jnp.float32
BF16 = jnp.bfloat16
MIB = 1024 * 1024
NT = (((1,), (1,)), ((), ()))
TN = (((0,), (0,)), ((), ()))


def iota(shape, dim):
    return lax.broadcasted_iota(jnp.int32, shape, dim)


def one_hot(cond):
    return jnp.where(cond, 1.0, 0.0).astype(BF16)


def pick(hot, rows):
    return jnp.dot(hot, rows, preferred_element_type=F32).astype(BF16)


def to_octets(out_ref, wide_ref, first, blocks):
    slots = blocks[0].shape[0]
    for i, block in enumerate(blocks):
        wide_ref[pl.ds(first + i, slots, stride=OCT), :] = block.astype(F32)
    out_ref[...] = wide_ref[...].astype(BF16)


def from_octets(in_ref, wide_ref, count):
    wide_ref[...] = in_ref[...].astype(F32)
    slots = in_ref.shape[0] // OCT
    return [wide_ref[pl.ds(i, slots, stride=OCT), :].astype(BF16) for i in range(count)]


def plan_kernel(n_dp, dest_ref, ids_ref, counts_ref, og_ref, pos_ref, og_moved_ref):
    tok = dest_ref.shape[1]
    slots = n_dp * CAP
    mine = lax.axis_index("dp")
    dest = dest_ref[...]
    counts = counts_ref[...]
    big_id = jnp.where(
        counts[:, 0:1] == BIG, 0, jnp.where(counts[:, 1:2] == BIG, 1, 2)
    )
    kept_class = jnp.where(ids_ref[...] == big_id, n_dp, n_dp + 1)
    group = jnp.where(dest == mine, kept_class, dest)
    n_rows = n_dp + 16
    row = iota((n_rows, tok), 0)
    member = row == group
    before = one_hot(iota((tok, tok), 0) < iota((tok, tok), 1))
    rank = jnp.dot(one_hot(member), before, preferred_element_type=F32)
    start = jnp.where(row < n_dp, CAP * row, jnp.where(row == n_dp, slots, slots + BIG))
    place = jnp.where(member, start.astype(F32) + rank, 0.0)
    pos = jnp.sum(place, axis=0, keepdims=True).astype(jnp.int32)
    pos_ref[...] = jnp.broadcast_to(pos, pos_ref.shape)
    rows = pick(one_hot(iota((slots, tok), 0) == pos), og_ref[...])
    for copy in range(og_moved_ref.shape[0]):
        og_moved_ref[copy] = rows


def pack_kernel(
    n_dp, pos_ref, og_ref, q_ref, k_ref, v_ref,
    send_ref, og_kept_ref, rows_kept_ref, used_ref, kept_used_ref, pos_col_ref, wide_ref,
):
    tok = og_ref.shape[0]
    slots = n_dp * CAP
    pos = pos_ref[0:1, :]
    q, k, v = q_ref[...], k_ref[...], v_ref[...]
    rows = jnp.concatenate([q, k, v], 1)
    slot_hot = one_hot(iota((slots, tok), 0) == pos)
    sent = jnp.dot(slot_hot, rows, preferred_element_type=F32)
    wide_ref[...] = jnp.zeros_like(wide_ref)
    to_octets(send_ref, wide_ref, 0, [sent[:, i * HD : (i + 1) * HD] for i in range(6)])
    kept_hot = one_hot(iota((KEPT, tok), 0) + slots == pos)
    og_kept_ref[...] = pick(kept_hot, og_ref[...])
    rows_kept_ref[...] = pick(kept_hot, rows)
    ones = jnp.ones((tok, HD), BF16)
    used_ref[...] = jnp.dot(slot_hot, ones, preferred_element_type=F32)
    kept_used_ref[...] = jnp.dot(kept_hot[BIG:], ones, preferred_element_type=F32)
    wide = jnp.broadcast_to(pos.astype(F32), (HD, tok))
    pos_col_ref[...] = jnp.transpose(wide).astype(jnp.int32)


def attend(q, k, v, g, valid, weight):
    scale = 1.0 / HD**0.5
    scores = lax.dot_general(k, q, NT, preferred_element_type=F32)
    if valid is not None:
        scores = jnp.where(valid, scores, -1e30)
    top = jnp.max(scores, axis=0, keepdims=True)
    raised = jnp.exp2((scores - top) * (scale * LOG2E))
    total = jnp.sum(raised, axis=0, keepdims=True)
    probs = raised * (1.0 / total)
    prob_grad = lax.dot_general(v, g, NT, preferred_element_type=F32)
    row_dot = jnp.sum(probs * prob_grad, axis=0, keepdims=True)
    scaled = probs * weight
    value_grad = jnp.dot(scaled.astype(BF16), g, preferred_element_type=F32)
    score_grad = (scaled * (prob_grad - row_dot)).astype(BF16)
    key_grad = jnp.dot(score_grad, q, preferred_element_type=F32) * scale
    query_grad = lax.dot_general(score_grad, k, TN, preferred_element_type=F32) * scale
    return query_grad.astype(BF16), key_grad.astype(BF16), value_grad.astype(BF16)


def block_dot(rows, w_ref, start):
    cols = rows.shape[1]
    weight = w_ref[:, pl.ds(pl.multiple_of(start, HD), cols)]
    return lax.dot_general(rows, weight, NT, preferred_element_type=F32)


def source_start(n_mp, me, away, feat):
    chips = n_mp // 2
    chip, core = me // 2, me % 2
    return (jnp.where(core == 0, chip - away, chip + away) + chips) % chips * (2 * feat)


def partial_kernel(n_mp, own_ref, *refs):
    *hop_refs, w_ref, w_pair_ref, acc_ref, w_late_ref = refs
    chunks = len(hop_refs) // 2
    feat = own_ref.shape[1]
    me = lax.axis_index("mp")
    third = pl.multiple_of(source_start(n_mp, me, 3, feat), HD)
    last = pl.multiple_of((me + n_mp // 2) % n_mp * feat, HD)
    for side, weight_ref in enumerate((w_ref, w_pair_ref)):
        row = 0
        for chunk in range(chunks):
            rows = hop_refs[chunk].shape[1]
            acc = block_dot(own_ref[row : row + rows], weight_ref, me * feat)
            for hop in range(2):
                block_ref = hop_refs[hop * chunks + chunk]
                start = source_start(n_mp, me, hop + 1, feat)
                for half in range(2):
                    acc = acc + block_dot(block_ref[half], weight_ref, start + half * feat)
            acc_ref[side, row : row + rows] = acc
            row += rows
        w_late_ref[side, :, : 2 * feat] = weight_ref[:, pl.ds(third, 2 * feat)]
        w_late_ref[side, :, 2 * feat :] = weight_ref[:, pl.ds(last, feat)]


def last_kernel(acc_ref, *refs):
    *hop_refs, w_late_ref, mine_ref, pair_ref = refs
    chunks = len(hop_refs) // 2
    feat = hop_refs[0].shape[2]
    for side, out in enumerate((mine_ref, pair_ref)):
        row = 0
        for chunk in range(chunks):
            hop3_ref, hop4_ref = hop_refs[chunk], hop_refs[chunks + chunk]
            rows = hop3_ref.shape[1]
            acc = acc_ref[side, row : row + rows]
            for part, block in enumerate((hop3_ref[0], hop3_ref[1], hop4_ref[0])):
                weight = w_late_ref[side, :, part * feat : (part + 1) * feat]
                acc = acc + lax.dot_general(block, weight, NT, preferred_element_type=F32)
            out[row : row + rows] = acc
            row += rows


def chips_kernel(n_mp, og_ref, w_ref, w_pair_ref, mine_ref, pair_ref):
    chips, _, feat = og_ref.shape
    core = lax.axis_index("mp") % 2
    for weight_ref, out in ((w_ref, mine_ref), (w_pair_ref, pair_ref)):
        acc = block_dot(og_ref[0], weight_ref, core * feat)
        for chip in range(1, chips):
            acc = acc + block_dot(og_ref[chip], weight_ref, (2 * chip + core) * feat)
        out[...] = acc


def moved_kernel(mine_ref, pair_ref, rows_ref, send_ref, wide_ref):
    grad = mine_ref[...] + pair_ref[...]
    wide_ref[...] = rows_ref[...].astype(F32)
    to_octets(send_ref, wide_ref, 6, [grad[:, :HD], grad[:, HD:]])


def remote_kernel(tok, img, rows_ref, valid_ref, send_ref, wide_ref):
    q0, q1, k0, k1, v0, v1, g0, g1 = from_octets(rows_ref, wide_ref, OCT)
    valid = valid_ref[:, 0:1]
    count = jnp.sum(valid, axis=0, keepdims=True)
    weight = tok / (img * count)
    mask = valid > 0.5
    dq0, dk0, dv0 = attend(q0, k0, v0, g0, mask, weight)
    dq1, dk1, dv1 = attend(q1, k1, v1, g1, mask, weight)
    wide_ref[...] = jnp.zeros_like(wide_ref)
    to_octets(send_ref, wide_ref, 0, [dq0, dq1, dk0, dk1, dv0, dv1])


def local_kernel(
    n_dp, tok, img, mine_ref, pair_ref, rows_ref, valid_ref, pos_ref, dq_ref, dk_ref, dv_ref
):
    slots = n_dp * CAP
    grad = (mine_ref[...] + pair_ref[...]).astype(BF16)
    valid = valid_ref[:, 0:1]
    count = jnp.sum(valid, axis=0, keepdims=True)
    images = (
        (slice(0, BIG), None, tok / (img * BIG)),
        (slice(BIG, KEPT), valid > 0.5, tok / (img * count)),
    )
    parts = []
    for head in range(2):
        lanes = slice(head * HD, (head + 1) * HD)
        pieces = []
        for span, mask, weight in images:
            q = rows_ref[span, head * HD : (head + 1) * HD]
            k = rows_ref[span, (2 + head) * HD : (3 + head) * HD]
            v = rows_ref[span, (4 + head) * HD : (5 + head) * HD]
            pieces.append(attend(q, k, v, grad[span, lanes], mask, weight))
        parts.append([jnp.concatenate(p, 0) for p in zip(*pieces)])
    pos = pos_ref[:, 0:1] - slots
    hot = one_hot(iota((tok, KEPT), 1) == pos)
    for name, out in enumerate((dq_ref, dk_ref, dv_ref)):
        out[...] = pick(hot, jnp.concatenate([parts[0][name], parts[1][name]], 1))


def merge_kernel(back_ref, pos_ref, q_ref, k_ref, v_ref, dq_ref, dk_ref, dv_ref, wide_ref):
    tok = q_ref.shape[0]
    slots = back_ref.shape[0] // OCT
    hot = one_hot(iota((tok, slots), 1) == pos_ref[:, 0:1])
    back = from_octets(back_ref, wide_ref, 6)
    for i, (kept_ref, out) in enumerate(((q_ref, dq_ref), (k_ref, dk_ref), (v_ref, dv_ref))):
        rows = jnp.concatenate(back[2 * i : 2 * i + 2], 1)
        out[...] = kept_ref[...] + pick(hot, rows)


def sds(shape, dtype):
    return jax.ShapeDtypeStruct(shape, dtype)


def call(kernel, ins, outs, name, vmem=56, flops=0, scratch=()):
    many = isinstance(outs, tuple)
    return pl.pallas_call(
        kernel,
        out_shape=outs,
        grid=(1,),
        in_specs=[whole(x) for x in ins],
        out_specs=tuple(whole(x) for x in outs) if many else whole(outs),
        scratch_shapes=scratch,
        **options(ins, outs if many else (outs,), name, vmem, flops),
    )(*ins)


def whole(x):
    zeros = (0,) * len(x.shape)
    return pl.BlockSpec(x.shape, lambda i: zeros)


def options(ins, outs, name, vmem, flops):
    size = sum(math.prod(x.shape) * x.dtype.itemsize for x in (*ins, *outs))
    return dict(
        compiler_params=pltpu.CompilerParams(vmem_limit_bytes=vmem * MIB),
        cost_estimate=pl.CostEstimate(flops=flops, bytes_accessed=size, transcendentals=0),
        name=name,
    )


def local(
    query_rows, key_rows, value_rows, out_grad, out_weight, destinations, image_ids, patch_counts
):
    tok, cols = query_rows.shape
    feat = out_grad.shape[1]
    n_dp, n_mp = lax.axis_size("dp"), lax.axis_size("mp")
    slots = n_dp * CAP
    img = patch_counts.shape[0]
    exch = slots * OCT
    wide = [pltpu.VMEM((exch, HD), F32)]
    swap = [(i, i ^ 1) for i in range(n_mp)]
    pairs = [[2 * i, 2 * i + 1] for i in range(n_mp // 2)]
    ring = [(i, (i + (2 if i % 2 == 0 else -2)) % n_mp) for i in range(n_mp)]
    same_core = [list(range(core, n_mp, 2)) for core in range(2)]

    def exchange(rows):
        shaped = rows.reshape(n_dp, CAP * OCT, HD)
        return lax.all_to_all(shaped, "dp", split_axis=0, concat_axis=0, tiled=True).reshape(rows.shape)

    def after(value, earlier):
        return lax.optimization_barrier((value, earlier))[0]

    def hop(block):
        return lax.ppermute(block, "mp", ring)

    def opposite(block):
        return hop(lax.dynamic_slice_in_dim(block, lax.axis_index("mp") % 2, 1, 0))

    def in_chunks(block):
        return [block[:, start : start + size] for start, size in CHUNKS]

    pair_weight = lax.ppermute(out_weight, "mp", swap)
    pos, og_moved = call(
        functools.partial(plan_kernel, n_dp),
        (destinations.reshape(1, tok), image_ids.reshape(1, tok), patch_counts.reshape(1, img), out_grad),
        (sds((8, tok), jnp.int32), sds((n_mp // 2, slots, feat), BF16)),
        "plan",
    )
    og_chips = lax.all_to_all(
        og_moved, "mp", split_axis=0, concat_axis=0, tiled=True, axis_index_groups=same_core
    )
    send, og_kept, rows_kept, used, kept_used, pos_col = call(
        functools.partial(pack_kernel, n_dp),
        (pos, out_grad, query_rows, key_rows, value_rows),
        (
            sds((exch, HD), BF16),
            sds((KEPT, feat), BF16),
            sds((KEPT, 3 * cols), BF16),
            sds((slots, HD), F32),
            sds((SMALL, HD), F32),
            sds((tok, HD), jnp.int32),
        ),
        "pack",
        scratch=wide,
    )
    kept_block = lax.all_gather(og_kept, "mp", axis=0, axis_index_groups=pairs)
    og_chips = after(og_chips, kept_block)
    kept1 = hop(after(kept_block, og_chips))
    mine, pair = call(
        functools.partial(chips_kernel, n_mp),
        (og_chips, out_weight, pair_weight),
        (sds((slots, cols), F32),) * 2,
        "chips",
        24,
    )
    pair = after(lax.ppermute(pair, "mp", swap), kept1)
    moved_send = call(
        moved_kernel,
        (mine, pair, send),
        sds((exch, HD), BF16),
        "moved",
        8,
        scratch=wide,
    )
    rows_in = exchange(moved_send)
    kept1 = in_chunks(after(kept1, moved_send))
    kept2 = [hop(x) for x in kept1]
    kept3 = [hop(x) for x in kept2]
    acc, w_late = call(
        functools.partial(partial_kernel, n_mp),
        (og_kept, *kept1, *kept2, out_weight, pair_weight),
        (sds((2, KEPT, cols), F32), sds((2, cols, 3 * feat), BF16)),
        "partial",
        56,
        2 * KEPT * n_mp * feat * cols,
    )
    for x in (acc, *kept3):
        rows_in = after(rows_in, x)
    back_send = call(
        functools.partial(remote_kernel, tok, img),
        (rows_in, used),
        sds((exch, HD), BF16),
        "remote",
        12,
        scratch=wide,
    )
    back = exchange(back_send)
    kept4 = [opposite(after(x, back_send)) for x in kept3]
    mine, pair = call(
        last_kernel, (acc, *kept3, *kept4, w_late), (sds((KEPT, cols), F32),) * 2, "last"
    )
    pair = lax.ppermute(pair, "mp", swap)
    kept_grads = call(
        functools.partial(local_kernel, n_dp, tok, img),
        (mine, pair, rows_kept, kept_used, pos_col),
        (sds((tok, cols), BF16),) * 3,
        "kept",
        24,
    )
    return call(
        merge_kernel,
        (back, pos_col) + kept_grads,
        (sds((tok, cols), BF16),) * 3,
        "merge",
        12,
        scratch=wide,
    )


def solution(mesh):
    rows = P("dp", "mp")
    return jax.shard_map(
        local,
        mesh=mesh,
        in_specs=(rows, rows, rows, rows, P("mp", None), P("dp"), P("dp"), P("dp")),
        out_specs=(rows, rows, rows),
        check_vma=False,
    )
```

```python
import functools
import math

import jax
import jax.numpy as jnp
from jax import lax
from jax.experimental import pallas as pl
from jax.experimental.pallas import tpu as pltpu
from jax.sharding import PartitionSpec as P

HD = 128
CAP = 3
BIG = 256
SMALL = 144
KEPT = BIG + SMALL
OCT = 8
LOG2E = 1.4426950408889634
F32 = jnp.float32
BF16 = jnp.bfloat16
MIB = 1024 * 1024
NT = (((1,), (1,)), ((), ()))
TN = (((0,), (0,)), ((), ()))


def iota(shape, dim):
    return lax.broadcasted_iota(jnp.int32, shape, dim)


def one_hot(cond):
    return jnp.where(cond, 1.0, 0.0).astype(BF16)


def pick(hot, rows):
    return jnp.dot(hot, rows, preferred_element_type=F32).astype(BF16)


def to_octets(out_ref, wide_ref, first, blocks):
    slots = blocks[0].shape[0]
    for i, block in enumerate(blocks):
        wide_ref[pl.ds(first + i, slots, stride=OCT), :] = block.astype(F32)
    out_ref[...] = wide_ref[...].astype(BF16)


def from_octets(in_ref, wide_ref, count):
    wide_ref[...] = in_ref[...].astype(F32)
    slots = in_ref.shape[0] // OCT
    return [wide_ref[pl.ds(i, slots, stride=OCT), :].astype(BF16) for i in range(count)]


def plan_kernel(n_dp, dest_ref, ids_ref, counts_ref, og_ref, pos_ref, og_moved_ref):
    tok = dest_ref.shape[1]
    slots = n_dp * CAP
    mine = lax.axis_index("dp")
    dest = dest_ref[...]
    counts = counts_ref[...]
    big_id = jnp.where(
        counts[:, 0:1] == BIG, 0, jnp.where(counts[:, 1:2] == BIG, 1, 2)
    )
    kept_class = jnp.where(ids_ref[...] == big_id, n_dp, n_dp + 1)
    group = jnp.where(dest == mine, kept_class, dest)
    n_rows = n_dp + 16
    row = iota((n_rows, tok), 0)
    member = row == group
    before = one_hot(iota((tok, tok), 0) < iota((tok, tok), 1))
    rank = jnp.dot(one_hot(member), before, preferred_element_type=F32)
    start = jnp.where(row < n_dp, CAP * row, jnp.where(row == n_dp, slots, slots + BIG))
    place = jnp.where(member, start.astype(F32) + rank, 0.0)
    pos = jnp.sum(place, axis=0, keepdims=True).astype(jnp.int32)
    pos_ref[...] = jnp.broadcast_to(pos, pos_ref.shape)
    rows = pick(one_hot(iota((slots, tok), 0) == pos), og_ref[...])
    for copy in range(og_moved_ref.shape[0]):
        og_moved_ref[copy] = rows


def pack_kernel(
    n_dp, pos_ref, og_ref, q_ref, k_ref, v_ref,
    send_ref, og_kept_ref, rows_kept_ref, used_ref, kept_used_ref, pos_col_ref, wide_ref,
):
    tok = og_ref.shape[0]
    slots = n_dp * CAP
    pos = pos_ref[0:1, :]
    q, k, v = q_ref[...], k_ref[...], v_ref[...]
    rows = jnp.concatenate([q, k, v], 1)
    slot_hot = one_hot(iota((slots, tok), 0) == pos)
    sent = jnp.dot(slot_hot, rows, preferred_element_type=F32)
    wide_ref[...] = jnp.zeros_like(wide_ref)
    to_octets(send_ref, wide_ref, 0, [sent[:, i * HD : (i + 1) * HD] for i in range(6)])
    kept_hot = one_hot(iota((KEPT, tok), 0) + slots == pos)
    og_kept_ref[...] = pick(kept_hot, og_ref[...])
    rows_kept_ref[...] = pick(kept_hot, rows)
    ones = jnp.ones((tok, HD), BF16)
    used_ref[...] = jnp.dot(slot_hot, ones, preferred_element_type=F32)
    kept_used_ref[...] = jnp.dot(kept_hot[BIG:], ones, preferred_element_type=F32)
    wide = jnp.broadcast_to(pos.astype(F32), (HD, tok))
    pos_col_ref[...] = jnp.transpose(wide).astype(jnp.int32)


def attend(q, k, v, g, valid, weight):
    scale = 1.0 / HD**0.5
    scores = lax.dot_general(k, q, NT, preferred_element_type=F32)
    if valid is not None:
        scores = jnp.where(valid, scores, -1e30)
    top = jnp.max(scores, axis=0, keepdims=True)
    raised = jnp.exp2((scores - top) * (scale * LOG2E))
    total = jnp.sum(raised, axis=0, keepdims=True)
    probs = raised * (1.0 / total)
    prob_grad = lax.dot_general(v, g, NT, preferred_element_type=F32)
    row_dot = jnp.sum(probs * prob_grad, axis=0, keepdims=True)
    scaled = probs * weight
    value_grad = jnp.dot(scaled.astype(BF16), g, preferred_element_type=F32)
    score_grad = (scaled * (prob_grad - row_dot)).astype(BF16)
    key_grad = jnp.dot(score_grad, q, preferred_element_type=F32) * scale
    query_grad = lax.dot_general(score_grad, k, TN, preferred_element_type=F32) * scale
    return query_grad.astype(BF16), key_grad.astype(BF16), value_grad.astype(BF16)


def parity_dot(block_ref, w_ref, parity):
    chips, rows, feat = block_ref.shape
    acc = jnp.zeros((rows, w_ref.shape[0]), F32)
    for chip in range(chips):
        start = pl.multiple_of((2 * chip + parity) * feat, HD)
        weight = w_ref[:, pl.ds(start, feat)]
        acc = acc + lax.dot_general(block_ref[chip], weight, NT, preferred_element_type=F32)
    return acc


def own_kernel(own_ref, w_ref, acc_ref):
    acc_ref[...] = parity_dot(own_ref, w_ref, lax.axis_index("mp") % 2)


def moved_kernel(acc_ref, pair_ref, w_ref, rows_hbm, send_ref, wide_ref, rows_ref, sem):
    fetch = pltpu.make_async_copy(rows_hbm, rows_ref, sem)
    fetch.start()
    grad = acc_ref[...] + parity_dot(pair_ref, w_ref, 1 - lax.axis_index("mp") % 2)
    fetch.wait()
    wide_ref[...] = rows_ref[...].astype(F32)
    to_octets(send_ref, wide_ref, 6, [grad[:, :HD], grad[:, HD:]])


def remote_kernel(tok, img, rows_ref, valid_ref, send_ref, wide_ref):
    q0, q1, k0, k1, v0, v1, g0, g1 = from_octets(rows_ref, wide_ref, OCT)
    valid = valid_ref[:, 0:1]
    count = jnp.sum(valid, axis=0, keepdims=True)
    weight = tok / (img * count)
    mask = valid > 0.5
    dq0, dk0, dv0 = attend(q0, k0, v0, g0, mask, weight)
    dq1, dk1, dv1 = attend(q1, k1, v1, g1, mask, weight)
    wide_ref[...] = jnp.zeros_like(wide_ref)
    to_octets(send_ref, wide_ref, 0, [dq0, dq1, dk0, dk1, dv0, dv1])


def project(og_ref, w_ref, acc_ref):
    blocks, _, cols = og_ref.shape

    @pl.when(pl.program_id(0) == 0)
    def _():
        acc_ref[...] = jnp.zeros_like(acc_ref)

    acc = acc_ref[...]
    for b in range(0, blocks, 2):
        rows = jnp.concatenate([og_ref[i] for i in range(b, min(b + 2, blocks))], 1)
        weight = w_ref[:, b * cols : b * cols + rows.shape[1]]
        acc = acc + lax.dot_general(rows, weight, NT, preferred_element_type=F32)
    acc_ref[...] = acc


def local_kernel(
    n_dp, tok, img, og_ref, w_ref, rows_ref, valid_ref, pos_ref,
    grads_ref, acc_ref,
):
    project(og_ref, w_ref, acc_ref)

    @pl.when(pl.program_id(0) == pl.num_programs(0) - 1)
    def _():
        slots = n_dp * CAP
        grad = acc_ref[...].astype(BF16)
        valid = valid_ref[:, 0:1]
        count = jnp.sum(valid, axis=0, keepdims=True)
        images = (
            (slice(0, BIG), None, tok / (img * BIG)),
            (slice(BIG, KEPT), valid > 0.5, tok / (img * count)),
        )
        parts = []
        for head in range(2):
            lanes = slice(head * HD, (head + 1) * HD)
            pieces = []
            for span, mask, weight in images:
                q = rows_ref[span, head * HD : (head + 1) * HD]
                k = rows_ref[span, (2 + head) * HD : (3 + head) * HD]
                v = rows_ref[span, (4 + head) * HD : (5 + head) * HD]
                pieces.append(attend(q, k, v, grad[span, lanes], mask, weight))
            parts.append([jnp.concatenate(p, 0) for p in zip(*pieces)])
        pos = pos_ref[:, 0:1] - slots
        hot = one_hot(iota((tok, KEPT), 1) == pos)
        for name in range(3):
            grads_ref[name] = pick(hot, jnp.concatenate([parts[0][name], parts[1][name]], 1))


def merge_kernel(back_ref, pos_ref, kept_ref, dq_ref, dk_ref, dv_ref, wide_ref):
    slots = back_ref.shape[0] // OCT
    hot = one_hot(iota((pos_ref.shape[0], slots), 1) == pos_ref[:, 0:1])
    back = from_octets(back_ref, wide_ref, 6)
    for i, out in enumerate((dq_ref, dk_ref, dv_ref)):
        out[...] = kept_ref[i] + pick(hot, jnp.concatenate(back[2 * i : 2 * i + 2], 1))


def sds(shape, dtype):
    return jax.ShapeDtypeStruct(shape, dtype)


def call(kernel, ins, outs, name, vmem=56, flops=0, scratch=(), in_hbm=()):
    many = isinstance(outs, tuple)
    return pl.pallas_call(
        kernel,
        out_shape=outs,
        grid=(1,),
        in_specs=[
            pl.BlockSpec(memory_space=pltpu.HBM) if i in in_hbm else whole(x)
            for i, x in enumerate(ins)
        ],
        out_specs=tuple(whole(x) for x in outs) if many else whole(outs),
        scratch_shapes=scratch,
        **options(ins, outs if many else (outs,), name, vmem, flops),
    )(*ins)


def whole(x):
    zeros = (0,) * len(x.shape)
    return pl.BlockSpec(x.shape, lambda i: zeros)


def options(ins, outs, name, vmem, flops):
    size = sum(math.prod(x.shape) * x.dtype.itemsize for x in (*ins, *outs))
    return dict(
        compiler_params=pltpu.CompilerParams(vmem_limit_bytes=vmem * MIB),
        cost_estimate=pl.CostEstimate(flops=flops, bytes_accessed=size, transcendentals=0),
        name=name,
    )


def local(
    query_rows, key_rows, value_rows, out_grad, out_weight, destinations, image_ids, patch_counts
):
    tok, cols = query_rows.shape
    feat = out_grad.shape[1]
    n_dp, n_mp = lax.axis_size("dp"), lax.axis_size("mp")
    slots = n_dp * CAP
    img = patch_counts.shape[0]
    exch = slots * OCT
    wide = [pltpu.VMEM((exch, HD), F32)]
    swap = [(i, i ^ 1) for i in range(n_mp)]
    same_core = [list(range(core, n_mp, 2)) for core in range(2)]

    def exchange(rows):
        shaped = rows.reshape(n_dp, CAP * OCT, HD)
        return lax.all_to_all(shaped, "dp", split_axis=0, concat_axis=0, tiled=True).reshape(rows.shape)

    def after(value, earlier):
        return lax.optimization_barrier((value, earlier))[0]

    pos, og_moved = call(
        functools.partial(plan_kernel, n_dp),
        (destinations.reshape(1, tok), image_ids.reshape(1, tok), patch_counts.reshape(1, img), out_grad),
        (sds((8, tok), jnp.int32), sds((n_mp // 2, slots, feat), BF16)),
        "plan",
    )
    og_chips = lax.all_to_all(
        og_moved, "mp", split_axis=0, concat_axis=0, tiled=True, axis_index_groups=same_core
    )
    og_pair = lax.ppermute(og_chips, "mp", swap)
    send, og_kept, rows_kept, used, kept_used, pos_col = call(
        functools.partial(pack_kernel, n_dp),
        (pos, out_grad, query_rows, key_rows, value_rows),
        (
            sds((exch, HD), BF16),
            sds((KEPT, feat), BF16),
            sds((KEPT, 3 * cols), BF16),
            sds((slots, HD), F32),
            sds((SMALL, HD), F32),
            sds((tok, HD), jnp.int32),
        ),
        "pack",
        scratch=wide,
    )
    kept_all = lax.all_gather(after(og_kept, og_chips), "mp", axis=0)
    own = call(
        own_kernel, (og_chips, out_weight), sds((slots, cols), F32), "own", 24, 10**9
    )
    moved_send = call(
        moved_kernel,
        (own, og_pair, out_weight, send),
        sds((exch, HD), BF16),
        "moved",
        24,
        scratch=wide + [pltpu.VMEM((exch, HD), BF16), pltpu.SemaphoreType.DMA],
        in_hbm=(3,),
    )
    rows_in = exchange(moved_send)
    back_send = call(
        functools.partial(remote_kernel, tok, img),
        (rows_in, used),
        sds((exch, HD), BF16),
        "remote",
        12,
        scratch=wide,
    )
    back = exchange(back_send)
    ins = (kept_all, out_weight, rows_kept, kept_used, pos_col)
    outs = sds((3, tok, cols), BF16)
    per_step = 4 if n_mp % 4 == 0 else 1
    kept_grads = pl.pallas_call(
        functools.partial(local_kernel, n_dp, tok, img),
        out_shape=outs,
        grid=(n_mp // per_step,),
        in_specs=[
            pl.BlockSpec((per_step, KEPT, feat), lambda i: (i, 0, 0)),
            pl.BlockSpec((cols, per_step * feat), lambda i: (0, i)),
            *(whole(x) for x in ins[2:]),
        ],
        out_specs=whole(outs),
        scratch_shapes=[pltpu.VMEM((KEPT, cols), F32)],
        **options(ins, (outs,), "kept", 56, 2 * KEPT * n_mp * feat * cols),
    )(*ins)
    return call(
        merge_kernel,
        (back, pos_col, kept_grads),
        (sds((tok, cols), BF16),) * 3,
        "merge",
        12,
        scratch=wide,
    )


def solution(mesh):
    rows = P("dp", "mp")
    return jax.shard_map(
        local,
        mesh=mesh,
        in_specs=(rows, rows, rows, rows, P("mp", None), P("dp"), P("dp"), P("dp")),
        out_specs=(rows, rows, rows),
        check_vma=False,
    )
```

```python
import functools
import math

import jax
import jax.numpy as jnp
from jax import lax
from jax.experimental import pallas as pl
from jax.experimental.pallas import tpu as pltpu
from jax.sharding import PartitionSpec as P

HD = 128
CAP = 3
BIG = 256
SMALL = 144
KEPT = BIG + SMALL
OCT = 8
LOG2E = 1.4426950408889634
F32 = jnp.float32
BF16 = jnp.bfloat16
MIB = 1024 * 1024
NT = (((1,), (1,)), ((), ()))
TN = (((0,), (0,)), ((), ()))


def iota(shape, dim):
    return lax.broadcasted_iota(jnp.int32, shape, dim)


def one_hot(cond):
    return jnp.where(cond, 1.0, 0.0).astype(BF16)


def pick(hot, rows):
    return jnp.dot(hot, rows, preferred_element_type=F32).astype(BF16)


def to_octets(out_ref, wide_ref, first, blocks):
    slots = blocks[0].shape[0]
    for i, block in enumerate(blocks):
        wide_ref[pl.ds(first + i, slots, stride=OCT), :] = block.astype(F32)
    out_ref[...] = wide_ref[...].astype(BF16)


def from_octets(in_ref, wide_ref, count):
    wide_ref[...] = in_ref[...].astype(F32)
    slots = in_ref.shape[0] // OCT
    return [wide_ref[pl.ds(i, slots, stride=OCT), :].astype(BF16) for i in range(count)]


def plan_kernel(n_dp, dest_ref, ids_ref, counts_ref, og_ref, pos_ref, og_moved_ref):
    tok = dest_ref.shape[1]
    slots = n_dp * CAP
    mine = lax.axis_index("dp")
    dest = dest_ref[...]
    counts = counts_ref[...]
    big_id = jnp.where(
        counts[:, 0:1] == BIG, 0, jnp.where(counts[:, 1:2] == BIG, 1, 2)
    )
    kept_class = jnp.where(ids_ref[...] == big_id, n_dp, n_dp + 1)
    group = jnp.where(dest == mine, kept_class, dest)
    n_rows = n_dp + 16
    row = iota((n_rows, tok), 0)
    member = row == group
    before = one_hot(iota((tok, tok), 0) < iota((tok, tok), 1))
    rank = jnp.dot(one_hot(member), before, preferred_element_type=F32)
    start = jnp.where(row < n_dp, CAP * row, jnp.where(row == n_dp, slots, slots + BIG))
    place = jnp.where(member, start.astype(F32) + rank, 0.0)
    pos = jnp.sum(place, axis=0, keepdims=True).astype(jnp.int32)
    pos_ref[...] = jnp.broadcast_to(pos, pos_ref.shape)
    rows = pick(one_hot(iota((slots, tok), 0) == pos), og_ref[...])
    for copy in range(og_moved_ref.shape[0]):
        og_moved_ref[copy] = rows


def pack_kernel(
    n_dp, pos_ref, og_ref, q_ref, k_ref, v_ref,
    send_ref, og_kept_ref, rows_kept_ref, used_ref, kept_used_ref, pos_col_ref, wide_ref,
):
    tok = og_ref.shape[0]
    slots = n_dp * CAP
    pos = pos_ref[0:1, :]
    q, k, v = q_ref[...], k_ref[...], v_ref[...]
    rows = jnp.concatenate([q, k, v], 1)
    slot_hot = one_hot(iota((slots, tok), 0) == pos)
    sent = jnp.dot(slot_hot, rows, preferred_element_type=F32)
    wide_ref[...] = jnp.zeros_like(wide_ref)
    to_octets(send_ref, wide_ref, 0, [sent[:, i * HD : (i + 1) * HD] for i in range(6)])
    kept_hot = one_hot(iota((KEPT, tok), 0) + slots == pos)
    og_kept_ref[...] = pick(kept_hot, og_ref[...])
    rows_kept_ref[...] = pick(kept_hot, rows)
    ones = jnp.ones((tok, HD), BF16)
    used_ref[...] = jnp.dot(slot_hot, ones, preferred_element_type=F32)
    kept_used_ref[...] = jnp.dot(kept_hot[BIG:], ones, preferred_element_type=F32)
    wide = jnp.broadcast_to(pos.astype(F32), (HD, tok))
    pos_col_ref[...] = jnp.transpose(wide).astype(jnp.int32)


def attend(q, k, v, g, valid, weight):
    scale = 1.0 / HD**0.5
    scores = lax.dot_general(k, q, NT, preferred_element_type=F32)
    if valid is not None:
        scores = jnp.where(valid, scores, -1e30)
    top = jnp.max(scores, axis=0, keepdims=True)
    raised = jnp.exp2((scores - top) * (scale * LOG2E))
    total = jnp.sum(raised, axis=0, keepdims=True)
    probs = raised * (1.0 / total)
    prob_grad = lax.dot_general(v, g, NT, preferred_element_type=F32)
    row_dot = jnp.sum(probs * prob_grad, axis=0, keepdims=True)
    scaled = probs * weight
    value_grad = jnp.dot(scaled.astype(BF16), g, preferred_element_type=F32)
    score_grad = (scaled * (prob_grad - row_dot)).astype(BF16)
    key_grad = jnp.dot(score_grad, q, preferred_element_type=F32) * scale
    query_grad = lax.dot_general(score_grad, k, TN, preferred_element_type=F32) * scale
    return query_grad.astype(BF16), key_grad.astype(BF16), value_grad.astype(BF16)


def parity_dot(block_ref, w_ref, parity):
    chips, rows, feat = block_ref.shape
    acc = jnp.zeros((rows, w_ref.shape[0]), F32)
    for chip in range(chips):
        start = pl.multiple_of((2 * chip + parity) * feat, HD)
        weight = w_ref[:, pl.ds(start, feat)]
        acc = acc + lax.dot_general(block_ref[chip], weight, NT, preferred_element_type=F32)
    return acc


def own_kernel(own_ref, w_ref, acc_ref):
    acc_ref[...] = parity_dot(own_ref, w_ref, lax.axis_index("mp") % 2)


def moved_kernel(acc_ref, pair_ref, w_ref, rows_hbm, send_ref, wide_ref, rows_ref, sem):
    fetch = pltpu.make_async_copy(rows_hbm, rows_ref, sem)
    fetch.start()
    grad = acc_ref[...] + parity_dot(pair_ref, w_ref, 1 - lax.axis_index("mp") % 2)
    fetch.wait()
    wide_ref[...] = rows_ref[...].astype(F32)
    to_octets(send_ref, wide_ref, 6, [grad[:, :HD], grad[:, HD:]])


def remote_kernel(tok, img, rows_ref, valid_ref, send_ref, wide_ref):
    q0, q1, k0, k1, v0, v1, g0, g1 = from_octets(rows_ref, wide_ref, OCT)
    valid = valid_ref[:, 0:1]
    count = jnp.sum(valid, axis=0, keepdims=True)
    weight = tok / (img * count)
    mask = valid > 0.5
    dq0, dk0, dv0 = attend(q0, k0, v0, g0, mask, weight)
    dq1, dk1, dv1 = attend(q1, k1, v1, g1, mask, weight)
    wide_ref[...] = jnp.zeros_like(wide_ref)
    to_octets(send_ref, wide_ref, 0, [dq0, dq1, dk0, dk1, dv0, dv1])


def project(og_ref, w_ref, acc_ref):
    blocks, _, cols = og_ref.shape

    @pl.when(pl.program_id(0) == 0)
    def _():
        acc_ref[...] = jnp.zeros_like(acc_ref)

    acc = acc_ref[...]
    for b in range(0, blocks, 2):
        rows = jnp.concatenate([og_ref[i] for i in range(b, min(b + 2, blocks))], 1)
        weight = w_ref[:, b * cols : b * cols + rows.shape[1]]
        acc = acc + lax.dot_general(rows, weight, NT, preferred_element_type=F32)
    acc_ref[...] = acc


def local_kernel(
    tok, img, og_ref, w_ref, rows_ref, valid_ref, grads_ref, acc_ref
):
    project(og_ref, w_ref, acc_ref)

    @pl.when(pl.program_id(0) == pl.num_programs(0) - 1)
    def _():
        grad = acc_ref[...].astype(BF16)
        valid = valid_ref[:, 0:1]
        count = jnp.sum(valid, axis=0, keepdims=True)
        images = (
            (slice(0, BIG), None, tok / (img * BIG)),
            (slice(BIG, KEPT), valid > 0.5, tok / (img * count)),
        )
        parts = []
        for head in range(2):
            lanes = slice(head * HD, (head + 1) * HD)
            pieces = []
            for span, mask, weight in images:
                q = rows_ref[span, head * HD : (head + 1) * HD]
                k = rows_ref[span, (2 + head) * HD : (3 + head) * HD]
                v = rows_ref[span, (4 + head) * HD : (5 + head) * HD]
                pieces.append(attend(q, k, v, grad[span, lanes], mask, weight))
            parts.append([jnp.concatenate(p, 0) for p in zip(*pieces)])
        for name in range(3):
            grads_ref[name] = jnp.concatenate([parts[0][name], parts[1][name]], 1)


def place_kernel(first, grads_ref, pos_ref, out_ref):
    shape = (pos_ref.shape[0], grads_ref.shape[1])
    hot = one_hot(iota(shape, 1) == pos_ref[:, 0:1] - first)
    for name in range(3):
        out_ref[name] = pick(hot, grads_ref[name])


def merge_kernel(back_ref, pos_ref, kept_ref, dq_ref, dk_ref, dv_ref, wide_ref):
    slots = back_ref.shape[0] // OCT
    hot = one_hot(iota((pos_ref.shape[0], slots), 1) == pos_ref[:, 0:1])
    back = from_octets(back_ref, wide_ref, 6)
    for i, out in enumerate((dq_ref, dk_ref, dv_ref)):
        out[...] = kept_ref[i] + pick(hot, jnp.concatenate(back[2 * i : 2 * i + 2], 1))


def sds(shape, dtype):
    return jax.ShapeDtypeStruct(shape, dtype)


def call(kernel, ins, outs, name, vmem=56, flops=0, scratch=(), in_hbm=()):
    many = isinstance(outs, tuple)
    return pl.pallas_call(
        kernel,
        out_shape=outs,
        grid=(1,),
        in_specs=[
            pl.BlockSpec(memory_space=pltpu.HBM) if i in in_hbm else whole(x)
            for i, x in enumerate(ins)
        ],
        out_specs=tuple(whole(x) for x in outs) if many else whole(outs),
        scratch_shapes=scratch,
        **options(ins, outs if many else (outs,), name, vmem, flops),
    )(*ins)


def whole(x):
    zeros = (0,) * len(x.shape)
    return pl.BlockSpec(x.shape, lambda i: zeros)


def options(ins, outs, name, vmem, flops):
    size = sum(math.prod(x.shape) * x.dtype.itemsize for x in (*ins, *outs))
    return dict(
        compiler_params=pltpu.CompilerParams(vmem_limit_bytes=vmem * MIB),
        cost_estimate=pl.CostEstimate(flops=flops, bytes_accessed=size, transcendentals=0),
        name=name,
    )


def local(
    query_rows, key_rows, value_rows, out_grad, out_weight, destinations, image_ids, patch_counts
):
    tok, cols = query_rows.shape
    feat = out_grad.shape[1]
    n_dp, n_mp = lax.axis_size("dp"), lax.axis_size("mp")
    slots = n_dp * CAP
    img = patch_counts.shape[0]
    exch = slots * OCT
    wide = [pltpu.VMEM((exch, HD), F32)]
    swap = [(i, i ^ 1) for i in range(n_mp)]
    same_core = [list(range(core, n_mp, 2)) for core in range(2)]

    def exchange(rows):
        shaped = rows.reshape(n_dp, CAP * OCT, HD)
        return lax.all_to_all(shaped, "dp", split_axis=0, concat_axis=0, tiled=True).reshape(rows.shape)

    def after(value, earlier):
        return lax.optimization_barrier((value, earlier))[0]

    pos, og_moved = call(
        functools.partial(plan_kernel, n_dp),
        (destinations.reshape(1, tok), image_ids.reshape(1, tok), patch_counts.reshape(1, img), out_grad),
        (sds((8, tok), jnp.int32), sds((n_mp // 2, slots, feat), BF16)),
        "plan",
    )
    og_chips = lax.all_to_all(
        og_moved, "mp", split_axis=0, concat_axis=0, tiled=True, axis_index_groups=same_core
    )
    og_pair = lax.ppermute(og_chips, "mp", swap)
    send, og_kept, rows_kept, used, kept_used, pos_col = call(
        functools.partial(pack_kernel, n_dp),
        (pos, out_grad, query_rows, key_rows, value_rows),
        (
            sds((exch, HD), BF16),
            sds((KEPT, feat), BF16),
            sds((KEPT, 3 * cols), BF16),
            sds((slots, HD), F32),
            sds((SMALL, HD), F32),
            sds((tok, HD), jnp.int32),
        ),
        "pack",
        scratch=wide,
    )
    kept_all = lax.all_gather(after(og_kept, og_chips), "mp", axis=0)
    own = call(
        own_kernel, (og_chips, out_weight), sds((slots, cols), F32), "own", 24, 10**9
    )
    moved_send = call(
        moved_kernel,
        (own, og_pair, out_weight, send),
        sds((exch, HD), BF16),
        "moved",
        24,
        scratch=wide + [pltpu.VMEM((exch, HD), BF16), pltpu.SemaphoreType.DMA],
        in_hbm=(3,),
    )
    rows_in = exchange(moved_send)
    back_send = call(
        functools.partial(remote_kernel, tok, img),
        (rows_in, used),
        sds((exch, HD), BF16),
        "remote",
        12,
        scratch=wide,
    )
    back = exchange(back_send)
    ins = (kept_all, out_weight, rows_kept, kept_used)
    outs = sds((3, KEPT, cols), BF16)
    per_step = 4 if n_mp % 4 == 0 else 1
    kept_grads = pl.pallas_call(
        functools.partial(local_kernel, tok, img),
        out_shape=outs,
        grid=(n_mp // per_step,),
        in_specs=[
            pl.BlockSpec((per_step, KEPT, feat), lambda i: (i, 0, 0)),
            pl.BlockSpec((cols, per_step * feat), lambda i: (0, i)),
            *(whole(x) for x in ins[2:]),
        ],
        out_specs=whole(outs),
        scratch_shapes=[pltpu.VMEM((KEPT, cols), F32)],
        **options(ins, (outs,), "kept", 56, 2 * KEPT * n_mp * feat * cols),
    )(*ins)
    kept_grads = call(
        functools.partial(place_kernel, slots),
        (kept_grads, pos_col),
        sds((3, tok, cols), BF16),
        "place",
        12,
    )
    return call(
        merge_kernel,
        (back, pos_col, kept_grads),
        (sds((tok, cols), BF16),) * 3,
        "merge",
        12,
        scratch=wide,
    )


def solution(mesh):
    rows = P("dp", "mp")
    return jax.shard_map(
        local,
        mesh=mesh,
        in_specs=(rows, rows, rows, rows, P("mp", None), P("dp"), P("dp"), P("dp")),
        out_specs=(rows, rows, rows),
        check_vma=False,
    )
```

```python
import functools
import math

import jax
import jax.numpy as jnp
from jax import lax
from jax.experimental import pallas as pl
from jax.experimental.pallas import tpu as pltpu
from jax.sharding import PartitionSpec as P

HD = 128
CAP = 3
BIG = 256
SMALL = 144
KEPT = BIG + SMALL
OCT = 8
LOG2E = 1.4426950408889634
F32 = jnp.float32
BF16 = jnp.bfloat16
MIB = 1024 * 1024
NT = (((1,), (1,)), ((), ()))
TN = (((0,), (0,)), ((), ()))


def iota(shape, dim):
    return lax.broadcasted_iota(jnp.int32, shape, dim)


def one_hot(cond):
    return jnp.where(cond, 1.0, 0.0).astype(BF16)


def pick(hot, rows):
    return jnp.dot(hot, rows, preferred_element_type=F32).astype(BF16)


def to_octets(out_ref, wide_ref, first, blocks):
    slots = blocks[0].shape[0]
    for i, block in enumerate(blocks):
        wide_ref[pl.ds(first + i, slots, stride=OCT), :] = block.astype(F32)
    out_ref[...] = wide_ref[...].astype(BF16)


def from_octets(in_ref, wide_ref, count):
    wide_ref[...] = in_ref[...].astype(F32)
    slots = in_ref.shape[0] // OCT
    return [wide_ref[pl.ds(i, slots, stride=OCT), :].astype(BF16) for i in range(count)]


def plan_kernel(n_dp, dest_ref, ids_ref, counts_ref, og_ref, pos_ref, og_moved_ref):
    tok = dest_ref.shape[1]
    slots = n_dp * CAP
    mine = lax.axis_index("dp")
    dest = dest_ref[...]
    counts = counts_ref[...]
    big_id = jnp.where(
        counts[:, 0:1] == BIG, 0, jnp.where(counts[:, 1:2] == BIG, 1, 2)
    )
    kept_class = jnp.where(ids_ref[...] == big_id, n_dp, n_dp + 1)
    group = jnp.where(dest == mine, kept_class, dest)
    n_rows = n_dp + 16
    row = iota((n_rows, tok), 0)
    member = row == group
    before = one_hot(iota((tok, tok), 0) < iota((tok, tok), 1))
    rank = jnp.dot(one_hot(member), before, preferred_element_type=F32)
    start = jnp.where(row < n_dp, CAP * row, jnp.where(row == n_dp, slots, slots + BIG))
    place = jnp.where(member, start.astype(F32) + rank, 0.0)
    pos = jnp.sum(place, axis=0, keepdims=True).astype(jnp.int32)
    pos_ref[...] = jnp.broadcast_to(pos, pos_ref.shape)
    rows = pick(one_hot(iota((slots, tok), 0) == pos), og_ref[...])
    for copy in range(og_moved_ref.shape[0]):
        og_moved_ref[copy] = rows


def pack_kernel(
    n_dp, pos_ref, og_ref, q_ref, k_ref, v_ref,
    send_ref, og_kept_ref, rows_kept_ref, used_ref, kept_used_ref, pos_col_ref, wide_ref,
):
    tok = og_ref.shape[0]
    slots = n_dp * CAP
    pos = pos_ref[0:1, :]
    q, k, v = q_ref[...], k_ref[...], v_ref[...]
    rows = jnp.concatenate([q, k, v], 1)
    slot_hot = one_hot(iota((slots, tok), 0) == pos)
    sent = jnp.dot(slot_hot, rows, preferred_element_type=F32)
    wide_ref[...] = jnp.zeros_like(wide_ref)
    to_octets(send_ref, wide_ref, 0, [sent[:, i * HD : (i + 1) * HD] for i in range(6)])
    kept_hot = one_hot(iota((KEPT, tok), 0) + slots == pos)
    og_kept_ref[...] = pick(kept_hot, og_ref[...])
    rows_kept_ref[...] = pick(kept_hot, rows)
    ones = jnp.ones((tok, HD), BF16)
    used_ref[...] = jnp.dot(slot_hot, ones, preferred_element_type=F32)
    kept_used_ref[...] = jnp.dot(kept_hot[BIG:], ones, preferred_element_type=F32)
    wide = jnp.broadcast_to(pos.astype(F32), (HD, tok))
    pos_col_ref[...] = jnp.transpose(wide).astype(jnp.int32)


def attend(q, k, v, g, valid, weight):
    scale = 1.0 / HD**0.5
    scores = lax.dot_general(k, q, NT, preferred_element_type=F32)
    if valid is not None:
        scores = jnp.where(valid, scores, -1e30)
    top = jnp.max(scores, axis=0, keepdims=True)
    raised = jnp.exp2((scores - top) * (scale * LOG2E))
    total = jnp.sum(raised, axis=0, keepdims=True)
    probs = raised * (1.0 / total)
    prob_grad = lax.dot_general(v, g, NT, preferred_element_type=F32)
    row_dot = jnp.sum(probs * prob_grad, axis=0, keepdims=True)
    scaled = probs * weight
    value_grad = jnp.dot(scaled.astype(BF16), g, preferred_element_type=F32)
    score_grad = (scaled * (prob_grad - row_dot)).astype(BF16)
    key_grad = jnp.dot(score_grad, q, preferred_element_type=F32) * scale
    query_grad = lax.dot_general(score_grad, k, TN, preferred_element_type=F32) * scale
    return query_grad.astype(BF16), key_grad.astype(BF16), value_grad.astype(BF16)


def parity_dot(block_ref, w_ref, parity):
    chips, rows, feat = block_ref.shape
    acc = jnp.zeros((rows, w_ref.shape[0]), F32)
    for first in range(0, chips, 2):
        pair = range(first, min(first + 2, chips))
        starts = [pl.multiple_of((2 * chip + parity) * feat, HD) for chip in pair]
        weight = jnp.concatenate([w_ref[:, pl.ds(start, feat)] for start in starts], 1)
        features = jnp.concatenate([block_ref[chip] for chip in pair], 1)
        acc = acc + lax.dot_general(features, weight, NT, preferred_element_type=F32)
    return acc


def own_kernel(own_ref, w_ref, acc_ref):
    acc_ref[...] = parity_dot(own_ref, w_ref, lax.axis_index("mp") % 2)


def moved_kernel(acc_ref, pair_ref, w_ref, rows_hbm, send_ref, wide_ref, rows_ref, sem):
    fetch = pltpu.make_async_copy(rows_hbm, rows_ref, sem)
    fetch.start()
    grad = acc_ref[...] + parity_dot(pair_ref, w_ref, 1 - lax.axis_index("mp") % 2)
    fetch.wait()
    wide_ref[...] = rows_ref[...].astype(F32)
    to_octets(send_ref, wide_ref, 6, [grad[:, :HD], grad[:, HD:]])


def remote_kernel(tok, img, rows_ref, valid_ref, send_ref, wide_ref):
    q0, q1, k0, k1, v0, v1, g0, g1 = from_octets(rows_ref, wide_ref, OCT)
    valid = valid_ref[:, 0:1]
    count = jnp.sum(valid, axis=0, keepdims=True)
    weight = tok / (img * count)
    mask = valid > 0.5
    dq0, dk0, dv0 = attend(q0, k0, v0, g0, mask, weight)
    dq1, dk1, dv1 = attend(q1, k1, v1, g1, mask, weight)
    wide_ref[...] = jnp.zeros_like(wide_ref)
    to_octets(send_ref, wide_ref, 0, [dq0, dq1, dk0, dk1, dv0, dv1])


def project(og_ref, w_ref, acc_ref):
    blocks, _, cols = og_ref.shape

    @pl.when(pl.program_id(0) == 0)
    def _():
        acc_ref[...] = jnp.zeros_like(acc_ref)

    acc = acc_ref[...]
    for b in range(0, blocks, 2):
        rows = jnp.concatenate([og_ref[i] for i in range(b, min(b + 2, blocks))], 1)
        weight = w_ref[:, b * cols : b * cols + rows.shape[1]]
        acc = acc + lax.dot_general(rows, weight, NT, preferred_element_type=F32)
    acc_ref[...] = acc


def local_kernel(
    tok, img, og_ref, w_ref, rows_ref, valid_ref, grads_ref, acc_ref
):
    project(og_ref, w_ref, acc_ref)

    @pl.when(pl.program_id(0) == pl.num_programs(0) - 1)
    def _():
        grad = acc_ref[...].astype(BF16)
        valid = valid_ref[:, 0:1]
        count = jnp.sum(valid, axis=0, keepdims=True)
        images = (
            (slice(0, BIG), None, tok / (img * BIG)),
            (slice(BIG, KEPT), valid > 0.5, tok / (img * count)),
        )
        parts = []
        for head in range(2):
            lanes = slice(head * HD, (head + 1) * HD)
            pieces = []
            for span, mask, weight in images:
                q = rows_ref[span, head * HD : (head + 1) * HD]
                k = rows_ref[span, (2 + head) * HD : (3 + head) * HD]
                v = rows_ref[span, (4 + head) * HD : (5 + head) * HD]
                pieces.append(attend(q, k, v, grad[span, lanes], mask, weight))
            parts.append([jnp.concatenate(p, 0) for p in zip(*pieces)])
        for name in range(3):
            grads_ref[name] = jnp.concatenate([parts[0][name], parts[1][name]], 1)


def place_kernel(first, grads_ref, pos_ref, out_ref):
    shape = (pos_ref.shape[0], grads_ref.shape[1])
    hot = one_hot(iota(shape, 1) == pos_ref[:, 0:1] - first)
    for name in range(3):
        out_ref[name] = pick(hot, grads_ref[name])


def merge_kernel(back_ref, pos_ref, kept_ref, dq_ref, dk_ref, dv_ref, wide_ref):
    slots = back_ref.shape[0] // OCT
    hot = one_hot(iota((pos_ref.shape[0], slots), 1) == pos_ref[:, 0:1])
    back = from_octets(back_ref, wide_ref, 6)
    for i, out in enumerate((dq_ref, dk_ref, dv_ref)):
        out[...] = kept_ref[i] + pick(hot, jnp.concatenate(back[2 * i : 2 * i + 2], 1))


def sds(shape, dtype):
    return jax.ShapeDtypeStruct(shape, dtype)


def call(kernel, ins, outs, name, vmem=56, flops=0, scratch=(), in_hbm=()):
    many = isinstance(outs, tuple)
    return pl.pallas_call(
        kernel,
        out_shape=outs,
        grid=(1,),
        in_specs=[
            pl.BlockSpec(memory_space=pltpu.HBM) if i in in_hbm else whole(x)
            for i, x in enumerate(ins)
        ],
        out_specs=tuple(whole(x) for x in outs) if many else whole(outs),
        scratch_shapes=scratch,
        **options(ins, outs if many else (outs,), name, vmem, flops),
    )(*ins)


def whole(x):
    zeros = (0,) * len(x.shape)
    return pl.BlockSpec(x.shape, lambda i: zeros)


def options(ins, outs, name, vmem, flops):
    size = sum(math.prod(x.shape) * x.dtype.itemsize for x in (*ins, *outs))
    return dict(
        compiler_params=pltpu.CompilerParams(vmem_limit_bytes=vmem * MIB),
        cost_estimate=pl.CostEstimate(flops=flops, bytes_accessed=size, transcendentals=0),
        name=name,
    )


def local(
    query_rows, key_rows, value_rows, out_grad, out_weight, destinations, image_ids, patch_counts
):
    tok, cols = query_rows.shape
    feat = out_grad.shape[1]
    n_dp, n_mp = lax.axis_size("dp"), lax.axis_size("mp")
    slots = n_dp * CAP
    img = patch_counts.shape[0]
    exch = slots * OCT
    wide = [pltpu.VMEM((exch, HD), F32)]
    swap = [(i, i ^ 1) for i in range(n_mp)]
    same_core = [list(range(core, n_mp, 2)) for core in range(2)]

    def exchange(rows):
        shaped = rows.reshape(n_dp, CAP * OCT, HD)
        return lax.all_to_all(shaped, "dp", split_axis=0, concat_axis=0, tiled=True).reshape(rows.shape)

    def after(value, earlier):
        return lax.optimization_barrier((value, earlier))[0]

    pos, og_moved = call(
        functools.partial(plan_kernel, n_dp),
        (destinations.reshape(1, tok), image_ids.reshape(1, tok), patch_counts.reshape(1, img), out_grad),
        (sds((8, tok), jnp.int32), sds((n_mp // 2, slots, feat), BF16)),
        "plan",
    )
    og_chips = lax.all_to_all(
        og_moved, "mp", split_axis=0, concat_axis=0, tiled=True, axis_index_groups=same_core
    )
    og_pair = lax.ppermute(og_chips, "mp", swap)
    send, og_kept, rows_kept, used, kept_used, pos_col = call(
        functools.partial(pack_kernel, n_dp),
        (pos, out_grad, query_rows, key_rows, value_rows),
        (
            sds((exch, HD), BF16),
            sds((KEPT, feat), BF16),
            sds((KEPT, 3 * cols), BF16),
            sds((slots, HD), F32),
            sds((SMALL, HD), F32),
            sds((tok, HD), jnp.int32),
        ),
        "pack",
        scratch=wide,
    )
    kept_all = lax.all_gather(after(og_kept, og_chips), "mp", axis=0)
    own = call(
        own_kernel, (og_chips, out_weight), sds((slots, cols), F32), "own", 24, 10**9
    )
    moved_send = call(
        moved_kernel,
        (own, og_pair, out_weight, send),
        sds((exch, HD), BF16),
        "moved",
        24,
        scratch=wide + [pltpu.VMEM((exch, HD), BF16), pltpu.SemaphoreType.DMA],
        in_hbm=(3,),
    )
    rows_in = exchange(moved_send)
    back_send = call(
        functools.partial(remote_kernel, tok, img),
        (rows_in, used),
        sds((exch, HD), BF16),
        "remote",
        12,
        scratch=wide,
    )
    back = exchange(back_send)
    ins = (kept_all, out_weight, rows_kept, kept_used)
    outs = sds((3, KEPT, cols), BF16)
    per_step = 4 if n_mp % 4 == 0 else 1
    kept_grads = pl.pallas_call(
        functools.partial(local_kernel, tok, img),
        out_shape=outs,
        grid=(n_mp // per_step,),
        in_specs=[
            pl.BlockSpec((per_step, KEPT, feat), lambda i: (i, 0, 0)),
            pl.BlockSpec((cols, per_step * feat), lambda i: (0, i)),
            *(whole(x) for x in ins[2:]),
        ],
        out_specs=whole(outs),
        scratch_shapes=[pltpu.VMEM((KEPT, cols), F32)],
        **options(ins, (outs,), "kept", 56, 2 * KEPT * n_mp * feat * cols),
    )(*ins)
    kept_grads = call(
        functools.partial(place_kernel, slots),
        (kept_grads, pos_col),
        sds((3, tok, cols), BF16),
        "place",
        12,
    )
    return call(
        merge_kernel,
        (back, pos_col, kept_grads),
        (sds((tok, cols), BF16),) * 3,
        "merge",
        12,
        scratch=wide,
    )


def solution(mesh):
    rows = P("dp", "mp")
    return jax.shard_map(
        local,
        mesh=mesh,
        in_specs=(rows, rows, rows, rows, P("mp", None), P("dp"), P("dp"), P("dp")),
        out_specs=(rows, rows, rows),
        check_vma=False,
    )
```
